512 devices in a mesh: shard: 128 (over z, y, core), tensor: 4 (over x).
Axes of the slice: x: 4, y: 4, z: 16, core: 2. Of those that a mesh axis runs over, the one named last changes fastest.
Arguments:
- attention_grad: bfloat16 [4, 12288, 768], P(None, 'shard', 'tensor'), may hold values from -500 to 500
- up_grad: bfloat16 [12288, 3072], P('shard', 'tensor'), may hold values from -500 to 500
- down_grad: bfloat16 [49152, 768], P('shard', 'tensor'), may hold values from -500 to 500
- attention_basis: float32 [4, 12288, 256], P(None, 'shard'), may hold values from -0.21875 to 0.21875
- up_basis: float32 [12288, 256], P('shard'), may hold values from -0.21875 to 0.21875
- down_basis: float32 [49152, 256], P('shard'), may hold values from -0.109375 to 0.109375
- attention_mean: float32 [4, 4096, 768], P(None, 'shard', 'tensor'), may hold values from -1.8 to 1.8
- attention_power: float32 [4, 4096, 768], P(None, 'shard', 'tensor'), may hold values from 0.05 to 1
- up_mean: float32 [4096, 3072], P('shard', 'tensor'), may hold values from -1.8 to 1.8
- up_power: float32 [4096, 3072], P('shard', 'tensor'), may hold values from 0.05 to 1
- down_mean: float32 [4096, 768], P('shard', 'tensor'), may hold values from -1.8 to 1.8
- down_power: float32 [4096, 768], P('shard', 'tensor'), may hold values from 0.05 to 1
- vector_grad: float32 [13, 12288], P(None, ('shard', 'tensor')), may hold values from -6 to 6
- vector_mean: float32 [13, 12288], P(None, ('shard', 'tensor')), may hold values from -1.8 to 1.8
- vector_power: float32 [13, 12288], P(None, ('shard', 'tensor')), may hold values from 0.05 to 1
Outputs:
- step_attention: float32 [4, 12288, 768], P(None, 'shard', 'tensor')
- step_up: float32 [12288, 3072], P('shard', 'tensor')
- step_down: float32 [49152, 768], P('shard', 'tensor')
- mean_attention: float32 [4, 4096, 768], P(None, 'shard', 'tensor')
- power_attention: float32 [4, 4096, 768], P(None, 'shard', 'tensor')
- mean_up: float32 [4096, 3072], P('shard', 'tensor')
- power_up: float32 [4096, 3072], P('shard', 'tensor')
- mean_down: float32 [4096, 768], P('shard', 'tensor')
- power_down: float32 [4096, 768], P('shard', 'tensor')
- basis_attention: float32 [4, 12288, 256], P(None, 'shard')
- basis_up: float32 [12288, 256], P('shard')
- basis_down: float32 [49152, 256], P('shard')
- step_vector: float32 [13, 12288], P(None, ('shard', 'tensor'))
- mean_vector: float32 [13, 12288], P(None, ('shard', 'tensor'))
- power_vector: float32 [13, 12288], P(None, ('shard', 'tensor'))
The draws below stay inside these ranges and needn't reach their ends.
All inputs are finite; a program needn't handle non-finite values.
Results may differ from the reference program's by a relative error of at most 0.0003.
Values sent between devices are 32-bit elements; how exact they have to be, the bound alone decides.
No kernel may reach another device: no remote copies, remote signals or barrier semaphores. Data moves between devices by JAX's collectives and lax.ppermute only.
A program may use at most 64 MiB of HBM per device.

```python
import math
import jax
import jax.numpy as jnp
from jax import lax

D = 768
FF = 3072
RANK = 256
MATS = 4
NS_STEPS = 3
STEP = 10
VROWS = 13
LAYERS = 16


def scaled_gradient(seed_key, lead_shape, row_count, column_count):
    subkeys = jax.random.split(seed_key, 3)
    full_shape = lead_shape + (LAYERS, row_count, column_count)
    row_shape = lead_shape + (LAYERS, row_count, 1)
    column_shape = lead_shape + (LAYERS, 1, column_count)
    row_scale = jnp.exp(jax.random.uniform(subkeys[1], row_shape, jnp.float32) * math.log(10.0))
    column_scale = jnp.exp(jax.random.uniform(subkeys[2], column_shape, jnp.float32) * math.log(10.0))
    layer_place = jnp.arange(LAYERS, dtype=jnp.float32).reshape((LAYERS, 1, 1)) / max(LAYERS - 1, 1)
    layer_scale = 1.0 + 2.0 * layer_place
    entries = jnp.clip(jax.random.normal(subkeys[0], full_shape, jnp.float32), -5.0, 5.0)
    values = entries * row_scale * column_scale * layer_scale * 0.1
    return values.reshape(lead_shape + (LAYERS * row_count, column_count))


def draw_attention_grad(key, part):
    return scaled_gradient(jax.random.fold_in(key, 11), (MATS,), D, D).astype(jnp.bfloat16)


def draw_up_grad(key, part):
    return scaled_gradient(jax.random.fold_in(key, 12), (), D, FF).astype(jnp.bfloat16)


def draw_down_grad(key, part):
    return scaled_gradient(jax.random.fold_in(key, 13), (), FF, D).astype(jnp.bfloat16)


def shard_levels(key, extent, cuts, smallest, high):
    factor_of = 1.0
    for position, shards_of in cuts:
        draws = jax.random.uniform(jax.random.fold_in(jax.random.fold_in(key, 6), position), (shards_of,), jnp.float32, smallest / len(cuts), high / len(cuts))
        factor_of = factor_of * jnp.repeat(jnp.exp(draws), extent[position] // shards_of).reshape((-1,) + (1,) * (len(extent) - 1 - position))
    return factor_of


def centred(own_key, shape, scale, bound, cuts=(), kind=jnp.bfloat16):
    loudness = shard_levels(own_key, shape, cuts, -0.22, 0.18) if cuts else 1.0
    values = jax.random.normal(own_key, shape, jnp.float32) * scale * loudness
    return jnp.minimum(jnp.maximum(values, -bound), bound).astype(kind)


def setup_inputs(seed: int = 0) -> dict:
    arg_keys = jax.random.split(jax.random.key(seed), 16)
    return {
        "attention_grad": draw_attention_grad(jax.random.fold_in(arg_keys[15], 71), 0),
        "up_grad": draw_up_grad(jax.random.fold_in(arg_keys[15], 71), 0),
        "down_grad": draw_down_grad(jax.random.fold_in(arg_keys[15], 71), 0),
        "attention_basis": centred(arg_keys[3], (MATS, LAYERS * D, RANK), D ** -0.5, 0.21875, ((1, 128),), jnp.float32),
        "up_basis": centred(arg_keys[4], (LAYERS * D, RANK), D ** -0.5, 0.21875, ((0, 128),), jnp.float32),
        "down_basis": centred(arg_keys[5], (LAYERS * FF, RANK), FF ** -0.5, 0.109375, ((0, 128),), jnp.float32),
        "attention_mean": centred(arg_keys[6], (MATS, LAYERS * RANK, D), 0.3, 1.8, ((1, 128), (2, 4)), jnp.float32),
        "attention_power": jnp.clip(jnp.exp(math.log(1.0) - 2.9957323 * jax.random.uniform(arg_keys[7], (MATS, LAYERS * RANK, D), jnp.float32) ** shard_levels(arg_keys[7], (MATS, LAYERS * RANK, D), ((1, 128), (2, 4)), -0.2, 0.2)), 0.05, 1.0),
        "up_mean": centred(arg_keys[8], (LAYERS * RANK, FF), 0.3, 1.8, ((0, 128), (1, 4)), jnp.float32),
        "up_power": jnp.clip(jnp.exp(math.log(1.0) - 2.9957323 * jax.random.uniform(arg_keys[9], (LAYERS * RANK, FF), jnp.float32) ** shard_levels(arg_keys[9], (LAYERS * RANK, FF), ((0, 128), (1, 4)), -0.2, 0.2)), 0.05, 1.0),
        "down_mean": centred(arg_keys[10], (LAYERS * RANK, D), 0.3, 1.8, ((0, 128), (1, 4)), jnp.float32),
        "down_power": jnp.clip(jnp.exp(math.log(1.0) - 2.9957323 * jax.random.uniform(arg_keys[11], (LAYERS * RANK, D), jnp.float32) ** shard_levels(arg_keys[11], (LAYERS * RANK, D), ((0, 128), (1, 4)), -0.2, 0.2)), 0.05, 1.0),
        "vector_grad": centred(arg_keys[12], (VROWS, LAYERS * D), 1.0, 6.0, ((1, 512),), jnp.float32),
        "vector_mean": centred(arg_keys[13], (VROWS, LAYERS * D), 0.3, 1.8, ((1, 512),), jnp.float32),
        "vector_power": jnp.clip(jnp.exp(math.log(1.0) - 2.9957323 * jax.random.uniform(arg_keys[14], (VROWS, LAYERS * D), jnp.float32) ** shard_levels(arg_keys[14], (VROWS, LAYERS * D), ((1, 512),), -0.2, 0.2)), 0.05, 1.0),
    }


quintic_one = 3.4445
quintic_two = -4.775
quintic_three = 2.0315
decay_first = 0.9
decay_second = 0.95
adam_epsilon = 1e-08
norm_epsilon = 1e-07
galore_scale = 0.25
clip_rms = 1.0

def highest(left_side, right_side):
    return jnp.dot(left_side, right_side, precision=lax.Precision.HIGHEST, preferred_element_type=jnp.float32)

def quintic(gram_matrix):
    square = highest(gram_matrix, gram_matrix)
    identity = jnp.eye(gram_matrix.shape[0], dtype=jnp.float32)
    return quintic_one * identity + quintic_two * gram_matrix + quintic_three * square

def adam_moments(gradient, mean_now, power_now):
    mean_next = decay_first * mean_now + (1.0 - decay_first) * gradient
    power_next = decay_second * power_now + (1.0 - decay_second) * gradient * gradient
    fix_first = 1.0 - decay_first ** STEP
    fix_second = 1.0 - decay_second ** STEP
    normed = mean_next / fix_first / (jnp.sqrt(power_next / fix_second) + adam_epsilon)
    return (normed, mean_next, power_next)

def refine(gradient, basis, mean_now, power_now, factor):
    gradient = gradient.astype(jnp.float32) * factor
    projected = highest(basis.T, gradient)
    normed, mean_next, power_next = adam_moments(projected, mean_now, power_now)
    update = galore_scale * highest(basis, normed)
    subspace = highest(gradient, projected.T)
    gram_matrix = highest(subspace.T, subspace)
    scale_now = 1.0 / (jnp.sqrt(jnp.trace(gram_matrix)) + norm_epsilon)
    frame = subspace * scale_now
    gram_matrix = gram_matrix * (scale_now * scale_now)
    for sweep_index in range(NS_STEPS):
        frame = highest(frame, quintic(gram_matrix))
        gram_matrix = highest(frame.T, frame)
    return (update, mean_next, power_next, frame)

def reference(attention_grad, up_grad, down_grad, attention_basis, up_basis, down_basis, attention_mean, attention_power, up_mean, up_power, down_mean, down_power, vector_grad, vector_mean, vector_power):
    total_squares = jnp.sum(jnp.square(attention_grad.astype(jnp.float32)))
    total_squares = total_squares + jnp.sum(jnp.square(up_grad.astype(jnp.float32)))
    total_squares = total_squares + jnp.sum(jnp.square(down_grad.astype(jnp.float32)))
    total_squares = total_squares + jnp.sum(vector_grad * vector_grad)
    entry_count = LAYERS * (MATS * D * D + 2 * D * FF + VROWS * D)
    clip_limit = jnp.float32(clip_rms * math.sqrt(entry_count))
    factor = clip_limit / jnp.maximum(jnp.sqrt(total_squares), clip_limit)
    head_lists = [[[], [], [], []] for matrix in range(MATS)]
    up_lists = [[], [], [], []]
    down_lists = [[], [], [], []]
    for layer in range(LAYERS):
        row_low = layer * D
        rank_low = layer * RANK
        ff_low = layer * FF
        for matrix in range(MATS):
            result = refine(attention_grad[matrix, row_low:row_low + D], attention_basis[matrix, row_low:row_low + D], attention_mean[matrix, rank_low:rank_low + RANK], attention_power[matrix, rank_low:rank_low + RANK], factor)
            for slot in range(4):
                head_lists[matrix][slot].append(result[slot])
        result = refine(up_grad[row_low:row_low + D], up_basis[row_low:row_low + D], up_mean[rank_low:rank_low + RANK], up_power[rank_low:rank_low + RANK], factor)
        for slot in range(4):
            up_lists[slot].append(result[slot])
        result = refine(down_grad[ff_low:ff_low + FF], down_basis[ff_low:ff_low + FF], down_mean[rank_low:rank_low + RANK], down_power[rank_low:rank_low + RANK], factor)
        for slot in range(4):
            down_lists[slot].append(result[slot])

    def heads(slot):
        return jnp.stack([jnp.concatenate(head_lists[matrix][slot], 0) for matrix in range(MATS)], 0)
    step_vector, mean_vector, power_vector = adam_moments(vector_grad * factor, vector_mean, vector_power)
    return (heads(0), jnp.concatenate(up_lists[0], 0), jnp.concatenate(down_lists[0], 0), heads(1), heads(2), jnp.concatenate(up_lists[1], 0), jnp.concatenate(up_lists[2], 0), jnp.concatenate(down_lists[1], 0), jnp.concatenate(down_lists[2], 0), heads(3), jnp.concatenate(up_lists[3], 0), jnp.concatenate(down_lists[3], 0), step_vector, mean_vector, power_vector)
```

```python
import math

import jax
import jax.numpy as jnp
from jax import lax
from jax.experimental import pallas as pl
from jax.experimental.pallas import tpu as pltpu
from jax.sharding import Mesh
from jax.sharding import PartitionSpec as P

NS_STEPS = 3
STEP = 10
SHARD = ("z", "y", "c")
SHARD_TENSOR = ("z", "y", "c", "x")
OWNERS = ("x", "c")
PIECE = 128
VMEM = pl.BlockSpec(memory_space=pltpu.VMEM)
SMEM = pl.BlockSpec(memory_space=pltpu.SMEM)

quintic_one = 3.4445
quintic_two = -4.775
quintic_three = 2.0315
decay_first = 0.9
decay_second = 0.95
adam_epsilon = 1e-08
norm_epsilon = 1e-07
galore_scale = 0.25
clip_rms = 1.0

CONTRACT_FIRST = (((0,), (0,)), ((), ()))
CONTRACT_LAST = (((1,), (1,)), ((), ()))
CONTRACT_PLAIN = (((1,), (0,)), ((), ()))


def highest(left, right, dims=CONTRACT_PLAIN):
    return lax.dot_general(
        left, right, dims, precision=lax.Precision.HIGHEST, preferred_element_type=jnp.float32
    )


def thirds(value):
    first = value.astype(jnp.bfloat16)
    rest = value - first.astype(jnp.float32)
    second = rest.astype(jnp.bfloat16)
    third = (rest - second.astype(jnp.float32)).astype(jnp.bfloat16)
    return first, second, third


def exact_left(value, gradient, dims):
    total = None
    for term in reversed(thirds(value)):
        product = lax.dot_general(term, gradient, dims, preferred_element_type=jnp.float32)
        total = product if total is None else total + product
    return total


def exact_right(gradient, value, dims):
    total = None
    for term in reversed(thirds(value)):
        product = lax.dot_general(gradient, term, dims, preferred_element_type=jnp.float32)
        total = product if total is None else total + product
    return total


def adam_moments(gradient, mean_now, power_now):
    mean_next = decay_first * mean_now + (1.0 - decay_first) * gradient
    power_next = decay_second * power_now + (1.0 - decay_second) * gradient * gradient
    fix_first = 1.0 - decay_first**STEP
    fix_second = 1.0 - decay_second**STEP
    normed = mean_next / fix_first / (jnp.sqrt(power_next / fix_second) + adam_epsilon)
    return (normed, mean_next, power_next)


def square_sum(value):
    return jnp.sum(jnp.sum(value * value, axis=1, keepdims=True), axis=0, keepdims=True)


def project_kernel(core, ag, ug, dg, ab, ub, db, vg, keep, send, whole):
    heads = ag.shape[0]
    pairs = [(ag[m], ab[m]) for m in range(heads)] + [(ug[...], ub[...]), (dg[...], db[...])]
    squares = square_sum(vg[...])
    column = 0
    parts = []
    for gradient, basis in pairs:
        parts.append(exact_left(basis, gradient, CONTRACT_FIRST))
        squares = squares + square_sum(gradient.astype(jnp.float32))
        column += gradient.shape[1]
    rank = whole.shape[0]
    parts.append(jnp.broadcast_to(squares, (rank, whole.shape[1] - column)))
    whole[...] = jnp.concatenate(parts, axis=1)
    block = keep.shape[1]
    mine = core[0]
    for row in range(keep.shape[0]):
        keep[row] = whole[pl.ds(pl.multiple_of((2 * row + mine) * block, block), block), :]
        send[row] = whole[pl.ds(pl.multiple_of((2 * row + 1 - mine) * block, block), block), :]


def sum_kernel(column, parts, total, copies, squares):
    value = parts[0]
    for row in range(1, parts.shape[0]):
        value = value + parts[row]
    total[...] = value
    for row in range(copies.shape[0]):
        copies[row] = value
    squares[...] = jnp.broadcast_to(value[0:1, column : column + 1][None], squares.shape)


def moments_kernel(
    limit, sums, squares, am, ap, um, up, dm, dp, vg, vm, vp,
    normed, am_out, ap_out, um_out, up_out, dm_out, dp_out, vs_out, vm_out, vp_out, factor_out,
):
    total = jnp.sum(squares[...], axis=0)[0:1, 0:1]
    factor = limit / jnp.maximum(jnp.sqrt(total), limit)
    factor_out[...] = jnp.broadcast_to(factor, factor_out.shape)
    heads = am.shape[0]
    width = am.shape[2]
    column = 0
    parts = []
    value = sums[...] * factor
    for m in range(heads):
        step, mean, power = adam_moments(value[:, column : column + width], am[m], ap[m])
        parts.append(step)
        am_out[m] = mean
        ap_out[m] = power
        column += width
    width = um.shape[1]
    step, mean, power = adam_moments(value[:, column : column + width], um[...], up[...])
    parts.append(step)
    um_out[...] = mean
    up_out[...] = power
    column += width
    width = dm.shape[1]
    step, mean, power = adam_moments(value[:, column : column + width], dm[...], dp[...])
    parts.append(step)
    dm_out[...] = mean
    dp_out[...] = power
    column += width
    parts.append(jnp.zeros((value.shape[0], value.shape[1] - column), jnp.float32))
    normed[...] = jnp.concatenate(parts, axis=1)
    step, mean, power = adam_moments(vg[...] * factor, vm[...], vp[...])
    vs_out[...] = step
    vm_out[...] = mean
    vp_out[...] = power


def subspace_kernel(core, own, other, ag, ug, dg, pieces, whole):
    block = own.shape[1]
    mine = core[0]
    for row in range(own.shape[0]):
        whole[pl.ds(pl.multiple_of((2 * row + mine) * block, block), block), :] = own[row]
        whole[pl.ds(pl.multiple_of((2 * row + 1 - mine) * block, block), block), :] = other[row]
    value = whole[...]
    heads = ag.shape[0]
    slot = 0
    column = 0
    for gradient in [ag[m] for m in range(heads)] + [ug[...], dg[...]]:
        rows, width = gradient.shape
        product = exact_right(gradient, value[:, column : column + width], CONTRACT_LAST)
        column += width
        for start in range(0, rows, PIECE):
            stop = min(rows, start + PIECE)
            pieces[slot, : stop - start, :] = product[start:stop]
            if stop - start < PIECE:
                pieces[slot, stop - start :, :] = jnp.zeros(
                    (PIECE - stop + start, product.shape[1]), jnp.float32
                )
            slot += 1


def gram_kernel(parts, rows_out, packed):
    tensors = parts.shape[0] // 2
    for core in range(2):
        value = parts[core]
        for t in range(1, tensors):
            value = value + parts[2 * t + core]
        rows_out[core * PIECE : (core + 1) * PIECE, :] = value
    rows = rows_out[...]
    gram = highest(rows, rows, CONTRACT_FIRST)
    half = gram.shape[0] // 2
    quarter = half // 2
    packed[:half, :] = gram[:half, :]
    packed[half:, :half] = gram[half : half + quarter, half:]
    packed[half:, half:] = gram[half + quarter :, half:]


def spread_kernel(first, second, third, copies):
    value = first[...] + (second[...] + third[...])
    for row in range(copies.shape[0]):
        copies[row] = value


def refine_kernel(packs, rows, factor, pieces):
    pack = packs[0]
    for row in range(1, packs.shape[0]):
        pack = pack + packs[row]
    half = pack.shape[1] // 2
    top = pack[:half, :]
    corner = jnp.concatenate([pack[half:, :half], pack[half:, half:]], axis=0)
    gram = jnp.concatenate(
        [top, jnp.concatenate([top[:, half:].T, corner], axis=1)], axis=0
    )
    size = gram.shape[0]
    identity = (
        lax.broadcasted_iota(jnp.int32, (size, size), 0)
        == lax.broadcasted_iota(jnp.int32, (size, size), 1)
    ).astype(jnp.float32)
    trace = jnp.sum(jnp.sum(gram * identity, axis=1, keepdims=True), axis=0, keepdims=True)
    squared = factor[0:1, 0:1] * factor[0:1, 0:1]
    scale = squared / (squared * jnp.sqrt(trace) + norm_epsilon)
    frame = rows[...] * scale
    gram = gram * (scale * scale)
    for sweep in range(NS_STEPS):
        square = highest(gram, gram)
        poly = quintic_one * identity + quintic_two * gram + quintic_three * square
        frame = highest(frame, poly)
        if sweep + 1 < NS_STEPS:
            gram = highest(poly, highest(gram, poly))
    for t in range(pieces.shape[0] // 2):
        for core in range(2):
            pieces[2 * t + core] = frame[core * PIECE : (core + 1) * PIECE, :]


def frames_kernel(pieces, attention, up, down):
    for m in range(attention.shape[0]):
        attention[m] = pieces[m, : attention.shape[1], :]
    slot = attention.shape[0]
    up[...] = pieces[slot, : up.shape[0], :]
    for k in range(down.shape[0] // PIECE):
        down[k * PIECE : (k + 1) * PIECE, :] = pieces[slot + 1 + k]


def update_kernel(normed, ab, ub, db, step_attention, step_up, step_down):
    value = normed[...]
    column = 0
    heads = ab.shape[0]
    width = step_attention.shape[2]
    for m in range(heads):
        step_attention[m] = galore_scale * highest(ab[m], value[:, column : column + width])
        column += width
    width = step_up.shape[1]
    step_up[...] = galore_scale * highest(ub[...], value[:, column : column + width])
    column += width
    width = step_down.shape[1]
    step_down[...] = galore_scale * highest(db[...], value[:, column : column + width])


def shape_of(*shape):
    return jax.ShapeDtypeStruct(shape, jnp.float32)


def call(kernel, operands, outs, scratch=(), scalar=False, flops=0):
    single = not isinstance(outs, (tuple, list))
    out_list = [outs] if single else list(outs)
    moved = sum(4 * math.prod(o.shape) for o in out_list)
    moved += sum(o.dtype.itemsize * o.size for o in operands)
    specs = [VMEM] * len(operands)
    if scalar:
        specs[0] = SMEM
    return pl.pallas_call(
        kernel,
        out_shape=outs,
        in_specs=specs,
        out_specs=VMEM if single else [VMEM] * len(out_list),
        scratch_shapes=list(scratch),
        compiler_params=pltpu.CompilerParams(vmem_limit_bytes=32 * 1024 * 1024),
        cost_estimate=pl.CostEstimate(flops=flops, bytes_accessed=moved, transcendentals=0),
    )(*operands)


def exchange(value, axes):
    return lax.all_to_all(value, axes, split_axis=0, concat_axis=0, tiled=True)


def on_device(ag, ug, dg, ab, ub, db, am, ap, um, up, dm, dp, vg, vm, vp):
    heads, rows, width = ag.shape
    rank = ab.shape[2]
    block = am.shape[1]
    columns = heads * width + ug.shape[1] + dg.shape[1]
    padded = -(-(columns + 1) // 128) * 128
    tensors = lax.axis_size("x")
    planes = lax.axis_size("z")
    members = lax.axis_size("y")
    owners = tensors * lax.axis_size("c")
    entries = (ag.size + ug.size + dg.size + vg.size) * planes * members * owners
    limit = float(clip_rms * math.sqrt(entries))
    core = lax.axis_index("c").astype(jnp.int32).reshape(1)
    f32 = jnp.float32

    keep, send = call(
        project_kernel,
        (core, ag, ug, dg, ab, ub, db, vg),
        (shape_of(members, block, padded), shape_of(members, block, padded)),
        scratch=[pltpu.VMEM((rank, padded), f32)],
        scalar=True,
    )
    swap = [(0, 1), (1, 0)]
    chip = keep + lax.ppermute(send, "c", swap)
    scattered = exchange(chip, "y")

    def sum_body(parts, total, copies, squares):
        sum_kernel(columns, parts, total, copies, squares)

    sums, copies, squares = call(
        sum_body,
        (scattered,),
        (
            shape_of(block, padded),
            shape_of(members, block, padded),
            shape_of(planes * tensors, 8, 128),
        ),
    )
    own = exchange(copies, "y")
    squares = exchange(squares, ("z", "x"))
    other = lax.ppermute(own, "c", swap)

    def moments_body(*refs):
        moments_kernel(limit, *refs)

    outs = call(
        moments_body,
        (sums, squares, am, ap, um, up, dm, dp, vg, vm, vp),
        [shape_of(block, padded)]
        + [shape_of(*v.shape) for v in (am, ap, um, up, dm, dp, vg, vm, vp)]
        + [shape_of(8, 128)],
    )
    normed, am2, ap2, um2, up2, dm2, dp2, vs2, vm2, vp2, factor = outs
    all_normed = lax.all_gather(normed, ("y", "c"), axis=0, tiled=True)

    pieces = call(
        subspace_kernel,
        (core, own, other, ag, ug, dg),
        shape_of(owners, PIECE, rank),
        scratch=[pltpu.VMEM((rank, padded), f32)],
        scalar=True,
    )
    parts = exchange(pieces, OWNERS)
    own_rows, packed = call(
        gram_kernel, (parts,), (shape_of(2 * PIECE, rank), shape_of(3 * rank // 4, rank))
    )
    first = owners - 3
    places = [(s % 2) * tensors + s // 2 for s in range(first, owners)]
    ring = [(places[k], places[(k + 1) % 3]) for k in range(3)]
    back = [(b, a) for a, b in ring]
    second = lax.ppermute(packed, ("c", "x"), ring)
    third = lax.ppermute(packed, ("c", "x"), back)
    packs = call(
        spread_kernel, (packed, second, third), shape_of(members, 3 * rank // 4, rank)
    )
    packs = exchange(packs, "y")
    frames = call(
        refine_kernel, (packs, own_rows, factor), shape_of(owners, PIECE, rank)
    )
    frames = exchange(frames, OWNERS)
    basis_attention, basis_up, basis_down = call(
        frames_kernel, (frames,), [shape_of(*v.shape) for v in (ab, ub, db)]
    )
    step_attention, step_up, step_down = call(
        update_kernel,
        (all_normed, ab, ub, db),
        [shape_of(*v.shape) for v in (ag, ug, dg)],
    )
    return (
        step_attention, step_up, step_down,
        am2, ap2, um2, up2, dm2, dp2,
        basis_attention, basis_up, basis_down,
        vs2, vm2, vp2,
    )


def solution(mesh):
    tensors = mesh.shape["tensor"]
    split = Mesh(mesh.devices.reshape(-1, 4, 2, tensors), SHARD_TENSOR)
    stacked = P(None, SHARD, "x")
    flat = P(SHARD, "x")
    vector = P(None, SHARD_TENSOR)
    bases = (P(None, SHARD, None), P(SHARD, None), P(SHARD, None))
    moments = (stacked, stacked, flat, flat, flat, flat)
    in_specs = (stacked, flat, flat) + bases + moments + (vector,) * 3
    out_specs = (stacked, flat, flat) + moments + bases + (vector,) * 3
    return jax.shard_map(
        on_device, mesh=split, in_specs=in_specs, out_specs=out_specs, check_vma=False
    )
```

```python
import math

import jax
import jax.numpy as jnp
from jax import lax
from jax.experimental import pallas as pl
from jax.experimental.pallas import tpu as pltpu
from jax.sharding import Mesh
from jax.sharding import PartitionSpec as P

NS_STEPS = 3
STEP = 10
SHARD = ("z", "y", "c")
SHARD_TENSOR = ("z", "y", "c", "x")
OWNERS = ("x", "c")
PIECE = 128
VMEM = pl.BlockSpec(memory_space=pltpu.VMEM)
SMEM = pl.BlockSpec(memory_space=pltpu.SMEM)

quintic_one = 3.4445
quintic_two = -4.775
quintic_three = 2.0315
decay_first = 0.9
decay_second = 0.95
adam_epsilon = 1e-08
norm_epsilon = 1e-07
galore_scale = 0.25
clip_rms = 1.0

CONTRACT_FIRST = (((0,), (0,)), ((), ()))
CONTRACT_LAST = (((1,), (1,)), ((), ()))
CONTRACT_MIXED = (((0,), (1,)), ((), ()))
CONTRACT_PLAIN = (((1,), (0,)), ((), ()))


def highest(left, right, dims=CONTRACT_PLAIN):
    return lax.dot_general(
        left, right, dims, precision=lax.Precision.HIGHEST, preferred_element_type=jnp.float32
    )


def thirds(value):
    first = value.astype(jnp.bfloat16)
    rest = value - first.astype(jnp.float32)
    second = rest.astype(jnp.bfloat16)
    third = (rest - second.astype(jnp.float32)).astype(jnp.bfloat16)
    return first, second, third


def exact_left(value, gradient, dims):
    total = None
    for term in reversed(thirds(value)):
        product = lax.dot_general(term, gradient, dims, preferred_element_type=jnp.float32)
        total = product if total is None else total + product
    return total


def exact_right(gradient, value, dims):
    total = None
    for term in reversed(thirds(value)):
        product = lax.dot_general(gradient, term, dims, preferred_element_type=jnp.float32)
        total = product if total is None else total + product
    return total


def adam_moments(gradient, mean_now, power_now):
    mean_next = decay_first * mean_now + (1.0 - decay_first) * gradient
    power_next = decay_second * power_now + (1.0 - decay_second) * gradient * gradient
    fix_first = 1.0 - decay_first**STEP
    fix_second = 1.0 - decay_second**STEP
    normed = mean_next / fix_first / (jnp.sqrt(power_next / fix_second) + adam_epsilon)
    return (normed, mean_next, power_next)


def square_sum(value):
    return jnp.sum(jnp.sum(value * value, axis=1, keepdims=True), axis=0, keepdims=True)


def project_kernel(core, ag, ug, dg_t, ab, ub, db, vg, keep, send, whole):
    heads = ag.shape[0]
    pairs = [(ag[m], ab[m], CONTRACT_FIRST) for m in range(heads)]
    pairs += [(ug[...], ub[...], CONTRACT_FIRST), (dg_t[...], db[...], CONTRACT_MIXED)]
    squares = square_sum(vg[...])
    column = 0
    parts = []
    for gradient, basis, dims in pairs:
        parts.append(exact_left(basis, gradient, dims))
        squares = squares + square_sum(gradient.astype(jnp.float32))
        column += parts[-1].shape[1]
    rank = whole.shape[0]
    parts.append(jnp.broadcast_to(squares, (rank, whole.shape[1] - column)))
    whole[...] = jnp.concatenate(parts, axis=1)
    block = keep.shape[1]
    mine = core[0]
    for row in range(keep.shape[0]):
        keep[row] = whole[pl.ds(pl.multiple_of((2 * row + mine) * block, block), block), :]
        send[row] = whole[pl.ds(pl.multiple_of((2 * row + 1 - mine) * block, block), block), :]


def widen_kernel(ag, ug, dg_t, upper, lower):
    heads, _, width = ag.shape
    parts = [ag[m].astype(jnp.float32) for m in range(heads)] + [ug[...].astype(jnp.float32)]
    upper[...] = jnp.concatenate(parts, axis=1)
    lower[...] = dg_t[...].astype(jnp.float32)


def chip_kernel(column, keep, received, chip, squares):
    chip[...] = keep[...] + received[...]
    squares[...] = jnp.broadcast_to(chip[0][0:1, column : column + 1], squares.shape)


def sum_kernel(parts, total, copies):
    value = parts[0]
    for row in range(1, parts.shape[0]):
        value = value + parts[row]
    total[...] = value
    for row in range(copies.shape[0]):
        copies[row] = value


def moments_kernel(
    limit, sums, squares, am, ap, um, up, dm, dp, vg, vm, vp,
    normed, am_out, ap_out, um_out, up_out, dm_out, dp_out, vs_out, vm_out, vp_out, factor_out,
):
    total = squares[0:1, 0:1]
    factor = limit / jnp.maximum(jnp.sqrt(total), limit)
    factor_out[...] = jnp.broadcast_to(factor, factor_out.shape)
    heads = am.shape[0]
    width = am.shape[2]
    column = 0
    parts = []
    value = sums[...] * factor
    for m in range(heads):
        step, mean, power = adam_moments(value[:, column : column + width], am[m], ap[m])
        parts.append(step)
        am_out[m] = mean
        ap_out[m] = power
        column += width
    width = um.shape[1]
    step, mean, power = adam_moments(value[:, column : column + width], um[...], up[...])
    parts.append(step)
    um_out[...] = mean
    up_out[...] = power
    column += width
    width = dm.shape[1]
    step, mean, power = adam_moments(value[:, column : column + width], dm[...], dp[...])
    parts.append(step)
    dm_out[...] = mean
    dp_out[...] = power
    column += width
    parts.append(jnp.zeros((value.shape[0], value.shape[1] - column), jnp.float32))
    normed[...] = jnp.concatenate(parts, axis=1)
    step, mean, power = adam_moments(vg[...] * factor, vm[...], vp[...])
    vs_out[...] = step
    vm_out[...] = mean
    vp_out[...] = power


def subspace_kernel(core, halves, ag, ug, dg_t, upper, lower, pieces):
    mine = core[0]
    value = jnp.concatenate([halves[row] for row in range(halves.shape[0])], axis=0)
    heads, _, width = ag.shape
    there = upper[...].astype(jnp.bfloat16)
    own = [ag[m] for m in range(heads)] + [ug[...], dg_t[...]]
    other = [there[:, m * width : (m + 1) * width] for m in range(heads)]
    other += [there[:, heads * width :], lower[...].astype(jnp.bfloat16)]
    for place, gradients in ((mine, own), (1 - mine, other)):
        place = pl.multiple_of(place * PIECE, PIECE)
        slot = 0
        column = 0
        for index, gradient in enumerate(gradients):
            dims = CONTRACT_MIXED if index == heads + 1 else CONTRACT_LAST
            columns = gradient.shape[0] if index == heads + 1 else gradient.shape[1]
            product = exact_right(gradient, value[:, column : column + columns], dims)
            column += columns
            rows = product.shape[0]
            if rows % PIECE:
                gap = jnp.zeros((PIECE - rows % PIECE, product.shape[1]), jnp.float32)
                product = jnp.concatenate([product, gap], axis=0)
            for start in range(0, product.shape[0], PIECE):
                pieces[slot, pl.ds(place, PIECE), :] = product[start : start + PIECE]
                slot += 1


def gram_kernel(parts, rows_out, packed):
    tensors = parts.shape[0] // 2
    halves = []
    for core in range(2):
        value = parts[core]
        for t in range(1, tensors):
            value = value + parts[2 * t + core]
        halves.append(value)
    rows = jnp.concatenate(halves, axis=1)
    rows_out[...] = rows
    gram = highest(rows, rows, CONTRACT_FIRST)
    half = gram.shape[0] // 2
    quarter = half // 2
    packed[:half, :] = gram[:half, :]
    packed[half:, :half] = gram[half : half + quarter, half:]
    packed[half:, half:] = gram[half + quarter :, half:]


def spread_kernel(first, second, third, copies):
    value = first[...] + (second[...] + third[...])
    for row in range(copies.shape[0]):
        copies[row] = value


def refine_kernel(members, packs, rows, factor, pieces):
    pack = packs[0]
    for row in range(1, packs.shape[0]):
        pack = pack + packs[row]
    half = pack.shape[1] // 2
    top = pack[:half, :]
    corner = jnp.concatenate([pack[half:, :half], pack[half:, half:]], axis=0)
    gram = jnp.concatenate(
        [top, jnp.concatenate([top[:, half:].T, corner], axis=1)], axis=0
    )
    size = gram.shape[0]
    identity = (
        lax.broadcasted_iota(jnp.int32, (size, size), 0)
        == lax.broadcasted_iota(jnp.int32, (size, size), 1)
    ).astype(jnp.float32)
    trace = jnp.sum(jnp.sum(gram * identity, axis=1, keepdims=True), axis=0, keepdims=True)
    squared = factor[0:1, 0:1] * factor[0:1, 0:1]
    scale = squared / (squared * jnp.sqrt(trace) + norm_epsilon)
    frame = rows[...] * scale
    gram = gram * (scale * scale)
    for sweep in range(NS_STEPS):
        square = highest(gram, gram)
        poly = quintic_one * identity + quintic_two * gram + quintic_three * square
        if sweep + 1 < NS_STEPS:
            frame = highest(frame, poly)
            gram = highest(poly, highest(gram, poly))
    block = size // (2 * members)
    order = [c * members + y for y in range(members) for c in range(2)]
    poly = jnp.concatenate([poly[:, k * block : (k + 1) * block] for k in order], axis=1)
    frame = highest(frame, poly)
    for t in range(pieces.shape[0] // 2):
        for core in range(2):
            pieces[2 * t + core] = frame[core * PIECE : (core + 1) * PIECE, :]


def frames_kernel(pieces, attention, up, down):
    for m in range(attention.shape[0]):
        attention[m] = pieces[m, : attention.shape[1], :]
    slot = attention.shape[0]
    up[...] = pieces[slot, : up.shape[0], :]
    for k in range(down.shape[0] // PIECE):
        down[k * PIECE : (k + 1) * PIECE, :] = pieces[slot + 1 + k]


def update_kernel(where, own, other, ab, ub, db, step_attention, step_up, step_down_t, whole):
    count, block, _ = own.shape
    mine = where[0]
    for shift in range(count):
        row = 2 * lax.rem(where[1] + (count - shift), count)
        whole[pl.ds(pl.multiple_of((row + mine) * block, block), block), :] = own[shift]
        whole[pl.ds(pl.multiple_of((row + 1 - mine) * block, block), block), :] = other[shift]
    value = whole[...]
    column = 0
    heads = ab.shape[0]
    width = step_attention.shape[2]
    for m in range(heads):
        step_attention[m] = galore_scale * highest(ab[m], value[:, column : column + width])
        column += width
    width = step_up.shape[1]
    step_up[...] = galore_scale * highest(ub[...], value[:, column : column + width])
    column += width
    width = step_down_t.shape[0]
    part = value[:, column : column + width]
    step_down_t[...] = galore_scale * highest(part, db[...], CONTRACT_MIXED)


def shape_of(*shape):
    return jax.ShapeDtypeStruct(shape, jnp.float32)


def call(kernel, operands, outs, scratch=(), scalar=False, flops=0, fetch=False, after=()):
    single = not isinstance(outs, (tuple, list))
    out_list = [outs] if single else list(outs)
    moved = sum(4 * math.prod(o.shape) for o in out_list)
    moved += sum(o.dtype.itemsize * o.size for o in operands)
    if fetch:
        specs = [pl.BlockSpec(o.shape, lambda i, n=o.ndim: (0,) * n) for o in operands]
    else:
        specs = [VMEM] * len(operands)
    if scalar:
        specs[0] = SMEM
    count = len(operands)
    operands = (*operands, *after)
    specs = specs + [pl.BlockSpec(memory_space=pl.ANY)] * len(after)

    def body(*refs):
        kernel(*refs[:count], *refs[count + len(after) :])

    return pl.pallas_call(
        body,
        out_shape=outs,
        grid=(1,) if fetch else (),
        in_specs=specs,
        out_specs=VMEM if single else [VMEM] * len(out_list),
        scratch_shapes=list(scratch),
        compiler_params=pltpu.CompilerParams(vmem_limit_bytes=32 * 1024 * 1024),
        cost_estimate=pl.CostEstimate(flops=flops, bytes_accessed=moved, transcendentals=0),
    )(*operands)


def sum_over(value, axis, masks):
    for mask in masks:
        pairs = [(k, k ^ mask) for k in range(lax.axis_size(axis))]
        value = value + lax.ppermute(value, axis, pairs)
    return value


def exchange(value, axes):
    return lax.all_to_all(value, axes, split_axis=0, concat_axis=0, tiled=True)


def on_device(ag, ug, dg, ab, ub, db, am, ap, um, up, dm, dp, vg, vm, vp):
    heads, rows, width = ag.shape
    rank = ab.shape[2]
    block = am.shape[1]
    columns = heads * width + ug.shape[1] + dg.shape[1]
    padded = -(-(columns + 1) // 128) * 128
    tensors = lax.axis_size("x")
    planes = lax.axis_size("z")
    members = lax.axis_size("y")
    owners = tensors * lax.axis_size("c")
    entries = (ag.size + ug.size + dg.size + vg.size) * planes * members * owners
    limit = float(clip_rms * math.sqrt(entries))
    core = lax.axis_index("c").astype(jnp.int32).reshape(1)
    f32 = jnp.float32

    dg_t = dg.T
    keep, send = call(
        project_kernel,
        (core, ag, ug, dg_t, ab, ub, db, vg),
        (shape_of(members, block, padded), shape_of(members, block, padded)),
        scratch=[pltpu.VMEM((rank, padded), f32)],
        scalar=True,
        fetch=True,
    )
    swap = [(0, 1), (1, 0)]

    def chip_body(*refs):
        chip_kernel(columns, *refs)

    chip, squares = call(
        chip_body,
        (keep, lax.ppermute(send, "c", swap)),
        (shape_of(members, block, padded), shape_of(8, 128)),
    )
    scattered = exchange(chip, "y")
    upper, lower = call(
        widen_kernel, (ag, ug, dg_t), (shape_of(rows, heads * width + ug.shape[1]), shape_of(*dg_t.shape))
    )
    upper = lax.ppermute(upper, "c", swap)
    lower = lax.ppermute(lower, "c", swap)
    squares = sum_over(squares, "z", [1 << k for k in range(planes.bit_length() - 1)])
    sums, copies = call(
        sum_kernel,
        (scattered,),
        (shape_of(block, padded), shape_of(members, block, padded)),
        after=(squares, upper, lower),
    )
    own = exchange(copies, "y")
    squares = sum_over(squares, "y", [1 << k for k in range(members.bit_length() - 1)])
    squares = sum_over(squares, "x", [1 << k for k in range(tensors.bit_length() - 1)])
    pieces = call(
        subspace_kernel,
        (core, own, ag, ug, dg_t, upper, lower),
        shape_of(owners, 2 * PIECE, rank // 2),
        scalar=True,
        after=(squares,),
    )

    def moments_body(*refs):
        moments_kernel(limit, *refs)

    outs = call(
        moments_body,
        (sums, squares, am, ap, um, up, dm, dp, vg, vm, vp),
        [shape_of(block, padded)]
        + [shape_of(*v.shape) for v in (am, ap, um, up, dm, dp, vg, vm, vp)]
        + [shape_of(8, 128)],
    )
    normed, am2, ap2, um2, up2, dm2, dp2, vs2, vm2, vp2, factor = outs
    normed_parts = [normed]
    for shift in range(1, members):
        pairs = [(k, (k + shift) % members) for k in range(members)]
        normed_parts.append(lax.ppermute(normed, "y", pairs))
    parts = exchange(pieces, OWNERS)
    own_rows, packed = call(
        gram_kernel,
        (parts,),
        (shape_of(2 * PIECE, rank), shape_of(3 * rank // 4, rank)),
        after=normed_parts[1:],
    )
    first = owners - 3
    places = [(s % 2) * tensors + s // 2 for s in range(first, owners)]
    ring = [(places[k], places[(k + 1) % 3]) for k in range(3)]
    back = [(b, a) for a, b in ring]
    second = lax.ppermute(packed, ("c", "x"), ring)
    third = lax.ppermute(packed, ("c", "x"), back)
    packs = call(
        spread_kernel, (packed, second, third), shape_of(members, 3 * rank // 4, rank)
    )
    packs = exchange(packs, "y")

    def refine_body(*refs):
        refine_kernel(members, *refs)

    frames = call(
        refine_body, (packs, own_rows, factor), shape_of(owners, PIECE, rank)
    )
    frames = exchange(frames, OWNERS)
    basis_attention, basis_up, basis_down = call(
        frames_kernel, (frames,), [shape_of(*v.shape) for v in (ab, ub, db)]
    )
    where = jnp.stack([lax.axis_index("c"), lax.axis_index("y")]).astype(jnp.int32)
    own_normed = jnp.stack(normed_parts)
    other_normed = lax.ppermute(own_normed, "c", swap)
    step_attention, step_up, step_down_t = call(
        update_kernel,
        (where, own_normed, other_normed, ab, ub, db),
        [shape_of(*v.shape) for v in (ag, ug, dg_t)],
        scratch=[pltpu.VMEM((rank, padded), f32)],
        scalar=True,
    )
    return (
        step_attention, step_up, step_down_t.T,
        am2, ap2, um2, up2, dm2, dp2,
        basis_attention, basis_up, basis_down,
        vs2, vm2, vp2,
    )


def solution(mesh):
    tensors = mesh.shape["tensor"]
    split = Mesh(mesh.devices.reshape(-1, 4, 2, tensors), SHARD_TENSOR)
    stacked = P(None, SHARD, "x")
    flat = P(SHARD, "x")
    vector = P(None, SHARD_TENSOR)
    bases = (P(None, SHARD, None), P(SHARD, None), P(SHARD, None))
    moments = (stacked, stacked, flat, flat, flat, flat)
    in_specs = (stacked, flat, flat) + bases + moments + (vector,) * 3
    out_specs = (stacked, flat, flat) + moments + bases + (vector,) * 3
    return jax.shard_map(
        on_device, mesh=split, in_specs=in_specs, out_specs=out_specs, check_vma=False
    )
```

```python
import math

import jax
import jax.numpy as jnp
from jax import lax
from jax.experimental import pallas as pl
from jax.experimental.pallas import tpu as pltpu
from jax.sharding import Mesh
from jax.sharding import PartitionSpec as P

NS_STEPS = 3
STEP = 10
SHARD = ("z", "y", "c")
SHARD_TENSOR = ("z", "y", "c", "x")
OWNERS = ("x", "c")
PIECE = 128
EXTRA = 8
VMEM = pl.BlockSpec(memory_space=pltpu.VMEM)
HBM = pl.BlockSpec(memory_space=pltpu.HBM)
SMEM = pl.BlockSpec(memory_space=pltpu.SMEM)

quintic_one = 3.4445
quintic_two = -4.775
quintic_three = 2.0315
decay_first = 0.9
decay_second = 0.95
adam_epsilon = 1e-08
norm_epsilon = 1e-07
galore_scale = 0.25
clip_rms = 1.0

CONTRACT_FIRST = (((0,), (0,)), ((), ()))
CONTRACT_LAST = (((1,), (1,)), ((), ()))
CONTRACT_MIXED = (((0,), (1,)), ((), ()))
CONTRACT_PLAIN = (((1,), (0,)), ((), ()))


def highest(left, right, dims=CONTRACT_PLAIN):
    return lax.dot_general(
        left, right, dims, precision=lax.Precision.HIGHEST, preferred_element_type=jnp.float32
    )


def thirds(value):
    first = value.astype(jnp.bfloat16)
    rest = value - first.astype(jnp.float32)
    second = rest.astype(jnp.bfloat16)
    third = (rest - second.astype(jnp.float32)).astype(jnp.bfloat16)
    return first, second, third


def exact_left(value, gradient, dims):
    total = None
    for term in reversed(thirds(value)):
        product = lax.dot_general(term, gradient, dims, preferred_element_type=jnp.float32)
        total = product if total is None else total + product
    return total


def exact_right(gradient, value, dims):
    total = None
    for term in reversed(thirds(value)):
        product = lax.dot_general(gradient, term, dims, preferred_element_type=jnp.float32)
        total = product if total is None else total + product
    return total


def adam_moments(gradient, mean_now, power_now):
    mean_next = decay_first * mean_now + (1.0 - decay_first) * gradient
    power_next = decay_second * power_now + (1.0 - decay_second) * gradient * gradient
    fix_first = 1.0 - decay_first**STEP
    fix_second = 1.0 - decay_second**STEP
    normed = mean_next / fix_first / (jnp.sqrt(power_next / fix_second) + adam_epsilon)
    return (normed, mean_next, power_next)


def square_sum(value):
    return jnp.sum(jnp.sum(value * value, axis=1, keepdims=True), axis=0, keepdims=True)


def project_kernel(core, *refs):
    count = 7
    sources = refs[:count]
    keep, send, whole = refs[count : count + 3]
    held = refs[count + 3 : count + 3 + count]
    done = refs[-1]
    copies = [
        pltpu.make_async_copy(source, target, done.at[index])
        for index, (source, target) in enumerate(zip(sources, held))
    ]
    for copy in copies:
        copy.start()
    ag, ug, dg_t, ab, ub, db, vg = held
    heads = ag.shape[0]
    for index in (0, 3):
        copies[index].wait()
    parts = []
    squares = jnp.zeros((1, 1), jnp.float32)
    for m in range(heads):
        gradient = ag[m]
        parts.append(exact_left(ab[m], gradient, CONTRACT_FIRST))
        squares = squares + square_sum(gradient.astype(jnp.float32))
    for index in (1, 4):
        copies[index].wait()
    gradient = ug[...]
    parts.append(exact_left(ub[...], gradient, CONTRACT_FIRST))
    squares = squares + square_sum(gradient.astype(jnp.float32))
    for index in (2, 5, 6):
        copies[index].wait()
    gradient = dg_t[...]
    parts.append(exact_left(db[...], gradient, CONTRACT_MIXED))
    squares = squares + square_sum(gradient.astype(jnp.float32)) + square_sum(vg[...])
    column = sum(part.shape[1] for part in parts)
    parts.append(jnp.broadcast_to(squares, (whole.shape[0], whole.shape[1] - column)))
    whole[...] = jnp.concatenate(parts, axis=1)
    block = keep.shape[1]
    mine = core[0]
    for row in range(keep.shape[0]):
        keep[row] = whole[pl.ds(pl.multiple_of((2 * row + mine) * block, block), block), :]
        send[row] = whole[pl.ds(pl.multiple_of((2 * row + 1 - mine) * block, block), block), :]


def widen_kernel(ag, ug, dg_t, am, ap, um, up, dm, dp, wide, pack):
    heads, rows, width = ag.shape
    parts = [ag[m].astype(jnp.float32) for m in range(heads)] + [ug[...].astype(jnp.float32)]
    wide[:rows, :] = jnp.concatenate(parts, axis=1)
    lower = dg_t[...].astype(jnp.float32)
    for k in range(lower.shape[0] // rows):
        start = k * lower.shape[1]
        wide[rows:, start : start + lower.shape[1]] = lower[k * rows : (k + 1) * rows, :]
    block = am.shape[1]
    for index, (first, second, third) in enumerate(((am, um, dm), (ap, up, dp))):
        parts = [first[m] for m in range(heads)] + [second[...], third[...]]
        column = sum(part.shape[1] for part in parts)
        parts.append(jnp.ones((block, pack.shape[1] - column), jnp.float32))
        pack[index * block : (index + 1) * block, :] = jnp.concatenate(parts, axis=1)


def chip_kernel(column, keep, received, chip, squares):
    chip[...] = keep[...] + received[...]
    squares[...] = jnp.broadcast_to(chip[0][0:1, column : column + 1], squares.shape)


def sum_kernel(parts, copies):
    value = parts[0]
    for row in range(1, parts.shape[0]):
        value = value + parts[row]
    for row in range(copies.shape[0]):
        copies[row] = value


def moments_kernel(
    where, factor, halves, *refs
):
    count = halves.shape[0]
    packs = refs[:count]
    vg, vm, vp, normed = refs[count : count + 4]
    am, ap, um, up, dm, dp, vs_out, vm_out, vp_out = refs[count + 4 :]
    block = halves.shape[1]
    scale = factor[0:1, 0:1]
    for shift in range(count):
        row = lax.rem(where[1] + (count - shift), count)
        step, mean, power = adam_moments(
            halves[row] * scale, packs[shift][:block, :], packs[shift][block:, :]
        )
        normed[shift] = step
        if shift == 0:
            for value, first, second, third in ((mean, am, um, dm), (power, ap, up, dp)):
                column = 0
                width = first.shape[2]
                for m in range(first.shape[0]):
                    first[m] = value[:, column : column + width]
                    column += width
                second[...] = value[:, column : column + second.shape[1]]
                column += second.shape[1]
                third[...] = value[:, column : column + third.shape[1]]
    step, mean, power = adam_moments(vg[...] * scale, vm[...], vp[...])
    vs_out[...] = step
    vm_out[...] = mean
    vp_out[...] = power


def subspace_kernel(core, halves, squares, ag, ug, dg_t, wide, pieces):
    mine = core[0]
    value = jnp.concatenate([halves[row] for row in range(halves.shape[0])], axis=0)
    heads, rows, width = ag.shape
    there = wide[...].astype(jnp.bfloat16)
    tall = dg_t.shape[1]
    own = [ag[m] for m in range(heads)] + [ug[...], dg_t[...]]
    other = [there[:rows, m * width : (m + 1) * width] for m in range(heads)]
    other += [there[:rows, heads * width :]]
    lower = [there[rows:, k * tall : (k + 1) * tall] for k in range(dg_t.shape[0] // rows)]
    other += [jnp.concatenate(lower, axis=0)]
    total = jnp.broadcast_to(squares[0:1, 0:1], (EXTRA, pieces.shape[2]))
    for place, gradients in ((mine, own), (1 - mine, other)):
        place = pl.multiple_of(place * (PIECE + EXTRA), 8)
        slot = 0
        column = 0
        for index, gradient in enumerate(gradients):
            dims = CONTRACT_MIXED if index == heads + 1 else CONTRACT_LAST
            columns = gradient.shape[0] if index == heads + 1 else gradient.shape[1]
            product = exact_right(gradient, value[:, column : column + columns], dims)
            column += columns
            size = product.shape[0]
            if size % PIECE:
                gap = jnp.zeros((PIECE - size % PIECE, product.shape[1]), jnp.float32)
                product = jnp.concatenate([product, gap], axis=0)
            for start in range(0, product.shape[0], PIECE):
                part = jnp.concatenate([product[start : start + PIECE], total], axis=0)
                pieces[slot, pl.ds(place, PIECE + EXTRA), :] = part
                slot += 1


def gram_kernel(parts, rows_out, packed):
    tensors = parts.shape[0] // 2
    halves = []
    for core in range(2):
        value = parts[core]
        for t in range(1, tensors):
            value = value + parts[2 * t + core]
        halves.append(value)
    total = halves[0][PIECE : PIECE + 1, 0:1]
    low = [half[:PIECE, :] for half in halves]
    high = [half[PIECE + EXTRA : 2 * PIECE + EXTRA, :] for half in halves]
    rows = jnp.concatenate(
        [jnp.concatenate(low, axis=1), jnp.concatenate(high, axis=1)], axis=0
    )
    rows_out[...] = rows
    gram = highest(rows, rows, CONTRACT_FIRST)
    half = gram.shape[0] // 2
    quarter = half // 2
    packed[:half, :] = gram[:half, :]
    packed[half : half + quarter, :half] = gram[half : half + quarter, half:]
    packed[half : half + quarter, half:] = gram[half + quarter :, half:]
    packed[half + quarter :, :] = jnp.broadcast_to(total, (EXTRA, packed.shape[1]))


def spread_kernel(first, second, third, copies):
    size = first.shape[0] - EXTRA
    value = first[:size, :] + (second[:size, :] + third[:size, :])
    for row in range(copies.shape[0]):
        copies[row, :size, :] = value
        copies[row, size:, :] = first[size:, :]


def refine_kernel(limit, members, packs, rows, pieces, factor_out):
    pack = packs[0]
    for row in range(1, packs.shape[0]):
        pack = pack + packs[row]
    half = pack.shape[1] // 2
    last = pack.shape[0] - EXTRA
    top = pack[:half, :]
    corner = jnp.concatenate([pack[half:last, :half], pack[half:last, half:]], axis=0)
    factor = limit / jnp.maximum(jnp.sqrt(pack[last : last + 1, 0:1]), limit)
    factor_out[...] = jnp.broadcast_to(factor, factor_out.shape)
    gram = jnp.concatenate(
        [top, jnp.concatenate([top[:, half:].T, corner], axis=1)], axis=0
    )
    size = gram.shape[0]
    identity = (
        lax.broadcasted_iota(jnp.int32, (size, size), 0)
        == lax.broadcasted_iota(jnp.int32, (size, size), 1)
    ).astype(jnp.float32)
    trace = jnp.sum(jnp.sum(gram * identity, axis=1, keepdims=True), axis=0, keepdims=True)
    squared = factor * factor
    scale = squared / (squared * jnp.sqrt(trace) + norm_epsilon)
    frame = rows[...] * scale
    gram = gram * (scale * scale)
    for sweep in range(NS_STEPS):
        square = highest(gram, gram)
        poly = quintic_one * identity + quintic_two * gram + quintic_three * square
        if sweep + 1 < NS_STEPS:
            frame = highest(frame, poly)
            gram = highest(poly, highest(gram, poly))
    block = size // (2 * members)
    order = [c * members + y for y in range(members) for c in range(2)]
    poly = jnp.concatenate([poly[:, k * block : (k + 1) * block] for k in order], axis=1)
    frame = highest(frame, poly)
    for t in range(pieces.shape[0] // 2):
        for core in range(2):
            pieces[2 * t + core] = frame[core * PIECE : (core + 1) * PIECE, :]


def frames_kernel(pieces, attention, up, down):
    for m in range(attention.shape[0]):
        attention[m] = pieces[m, : attention.shape[1], :]
    slot = attention.shape[0]
    up[...] = pieces[slot, : up.shape[0], :]
    for k in range(down.shape[0] // PIECE):
        down[k * PIECE : (k + 1) * PIECE, :] = pieces[slot + 1 + k]


def update_kernel(where, own, other, ab, ub, db, step_attention, step_up, step_down_t, whole):
    count, block, _ = own.shape
    mine = where[0]
    for shift in range(count):
        row = 2 * lax.rem(where[1] + (count - shift), count)
        whole[pl.ds(pl.multiple_of((row + mine) * block, block), block), :] = own[shift]
        whole[pl.ds(pl.multiple_of((row + 1 - mine) * block, block), block), :] = other[shift]
    value = whole[...]
    column = 0
    heads = ab.shape[0]
    width = step_attention.shape[2]
    for m in range(heads):
        step_attention[m] = galore_scale * highest(ab[m], value[:, column : column + width])
        column += width
    width = step_up.shape[1]
    step_up[...] = galore_scale * highest(ub[...], value[:, column : column + width])
    column += width
    width = step_down_t.shape[0]
    part = value[:, column : column + width]
    step_down_t[...] = galore_scale * highest(part, db[...], CONTRACT_MIXED)


def shape_of(*shape):
    return jax.ShapeDtypeStruct(shape, jnp.float32)


def call(kernel, operands, outs, scratch=(), scalar=False, flops=0, fetch=False, after=()):
    single = not isinstance(outs, (tuple, list))
    out_list = [outs] if single else list(outs)
    moved = sum(4 * math.prod(o.shape) for o in out_list)
    moved += sum(o.dtype.itemsize * o.size for o in operands)
    specs = [HBM if fetch else VMEM] * len(operands)
    if scalar:
        specs[0] = SMEM
    count = len(operands)
    operands = (*operands, *after)
    specs = specs + [pl.BlockSpec(memory_space=pl.ANY)] * len(after)

    def body(*refs):
        kernel(*refs[:count], *refs[count + len(after) :])

    return pl.pallas_call(
        body,
        out_shape=outs,
        in_specs=specs,
        out_specs=VMEM if single else [VMEM] * len(out_list),
        scratch_shapes=list(scratch),
        compiler_params=pltpu.CompilerParams(vmem_limit_bytes=32 * 1024 * 1024),
        cost_estimate=pl.CostEstimate(flops=flops, bytes_accessed=moved, transcendentals=0),
    )(*operands)


def sum_over(value, axis, masks):
    total = value
    for mask in masks:
        pairs = [(k, k ^ mask) for k in range(lax.axis_size(axis))]
        total = total + lax.ppermute(value, axis, pairs)
    return total


def exchange(value, axes):
    return lax.all_to_all(value, axes, split_axis=0, concat_axis=0, tiled=True)


def on_device(ag, ug, dg, ab, ub, db, am, ap, um, up, dm, dp, vg, vm, vp):
    heads, rows, width = ag.shape
    rank = ab.shape[2]
    block = am.shape[1]
    columns = heads * width + ug.shape[1] + dg.shape[1]
    padded = -(-(columns + 1) // 128) * 128
    tensors = lax.axis_size("x")
    planes = lax.axis_size("z")
    members = lax.axis_size("y")
    owners = tensors * lax.axis_size("c")
    entries = (ag.size + ug.size + dg.size + vg.size) * planes * members * owners
    limit = float(clip_rms * math.sqrt(entries))
    where = jnp.stack([lax.axis_index("c"), lax.axis_index("y")]).astype(jnp.int32)
    f32 = jnp.float32

    dg_t = dg.T
    first_operands = (ag, ug, dg_t, ab, ub, db, vg)
    keep, send = call(
        project_kernel,
        (where, *first_operands),
        (shape_of(members, block, padded), shape_of(members, block, padded)),
        scratch=[pltpu.VMEM((rank, padded), f32)]
        + [pltpu.VMEM(o.shape, o.dtype) for o in first_operands]
        + [pltpu.SemaphoreType.DMA((len(first_operands),))],
        scalar=True,
        fetch=True,
    )
    swap = [(0, 1), (1, 0)]

    def chip_body(*refs):
        chip_kernel(columns, *refs)

    chip, squares = call(
        chip_body,
        (keep, lax.ppermute(send, "c", swap)),
        (shape_of(members, block, padded), shape_of(8, 128)),
    )
    scattered = exchange(chip, "y")
    wide, pack = call(
        widen_kernel,
        (ag, ug, dg_t, am, ap, um, up, dm, dp),
        (shape_of(2 * rows, heads * width + ug.shape[1]), shape_of(2 * block, padded)),
    )
    wide = lax.ppermute(wide, "c", swap)
    low = [k for k in range(1, min(4, planes))]
    high = [4 * k for k in range(1, planes // 4)]
    squares = sum_over(squares, "z", low)
    copies = call(
        sum_kernel, (scattered,), shape_of(members, block, padded), after=(squares, wide)
    )
    own = exchange(copies, "y")
    squares = sum_over(squares, "z", high)
    pieces = call(
        subspace_kernel,
        (where, own, squares, ag, ug, dg_t, wide),
        shape_of(owners, 2 * (PIECE + EXTRA), rank // 2),
        scalar=True,
    )
    packs = [pack]
    for shift in range(1, members):
        pairs = [(k, (k + shift) % members) for k in range(members)]
        packs.append(lax.ppermute(pack, "y", pairs))

    parts = exchange(pieces, OWNERS)
    packed_rows = 3 * rank // 4 + EXTRA
    own_rows, packed = call(
        gram_kernel,
        (parts,),
        (shape_of(2 * PIECE, rank), shape_of(packed_rows, rank)),
        after=packs[1:],
    )
    first = owners - 3
    places = [(s % 2) * tensors + s // 2 for s in range(first, owners)]
    ring = [(places[k], places[(k + 1) % 3]) for k in range(3)]
    back = [(b, a) for a, b in ring]
    second = lax.ppermute(packed, ("c", "x"), ring)
    third = lax.ppermute(packed, ("c", "x"), back)
    grams = call(spread_kernel, (packed, second, third), shape_of(members, packed_rows, rank))
    grams = exchange(grams, "y")

    def refine_body(*refs):
        refine_kernel(limit, members, *refs)

    frames, factor = call(
        refine_body,
        (grams, own_rows),
        (shape_of(owners, PIECE, rank), shape_of(8, 128)),
    )
    frames = exchange(frames, OWNERS)
    own_normed, am2, ap2, um2, up2, dm2, dp2, vs2, vm2, vp2 = call(
        moments_kernel,
        (where, factor, own, *packs, vg, vm, vp),
        [shape_of(members, block, padded)]
        + [shape_of(*v.shape) for v in (am, ap, um, up, dm, dp, vg, vm, vp)],
        scalar=True,
    )
    other_normed = lax.ppermute(own_normed, "c", swap)
    step_attention, step_up, step_down_t = call(
        update_kernel,
        (where, own_normed, other_normed, ab, ub, db),
        [shape_of(*v.shape) for v in (ag, ug, dg_t)],
        scratch=[pltpu.VMEM((rank, padded), f32)],
        scalar=True,
    )
    basis_attention, basis_up, basis_down = call(
        frames_kernel, (frames,), [shape_of(*v.shape) for v in (ab, ub, db)]
    )
    return (
        step_attention, step_up, step_down_t.T,
        am2, ap2, um2, up2, dm2, dp2,
        basis_attention, basis_up, basis_down,
        vs2, vm2, vp2,
    )


def solution(mesh):
    tensors = mesh.shape["tensor"]
    split = Mesh(mesh.devices.reshape(-1, 4, 2, tensors), SHARD_TENSOR)
    stacked = P(None, SHARD, "x")
    flat = P(SHARD, "x")
    vector = P(None, SHARD_TENSOR)
    bases = (P(None, SHARD, None), P(SHARD, None), P(SHARD, None))
    moments = (stacked, stacked, flat, flat, flat, flat)
    in_specs = (stacked, flat, flat) + bases + moments + (vector,) * 3
    out_specs = (stacked, flat, flat) + moments + bases + (vector,) * 3
    return jax.shard_map(
        on_device, mesh=split, in_specs=in_specs, out_specs=out_specs, check_vma=False
    )
```

```python
import math

import jax
import jax.numpy as jnp
from jax import lax
from jax.experimental import pallas as pl
from jax.experimental.pallas import tpu as pltpu
from jax.sharding import Mesh
from jax.sharding import PartitionSpec as P

NS_STEPS = 3
STEP = 10
SHARD = ("z", "y", "c")
SHARD_TENSOR = ("z", "y", "c", "x")
OWNERS = ("x", "c")
PIECE = 128
VMEM = pl.BlockSpec(memory_space=pltpu.VMEM)
HBM = pl.BlockSpec(memory_space=pltpu.HBM)
SMEM = pl.BlockSpec(memory_space=pltpu.SMEM)

quintic_one = 3.4445
quintic_two = -4.775
quintic_three = 2.0315
decay_first = 0.9
decay_second = 0.95
adam_epsilon = 1e-08
norm_epsilon = 1e-07
galore_scale = 0.25
clip_rms = 1.0

CONTRACT_FIRST = (((0,), (0,)), ((), ()))
CONTRACT_LAST = (((1,), (1,)), ((), ()))
CONTRACT_MIXED = (((0,), (1,)), ((), ()))
CONTRACT_PLAIN = (((1,), (0,)), ((), ()))


def highest(left, right, dims=CONTRACT_PLAIN):
    return lax.dot_general(
        left, right, dims, precision=lax.Precision.HIGHEST, preferred_element_type=jnp.float32
    )


def halves_of(value):
    first = value.astype(jnp.bfloat16)
    return first, (value - first.astype(jnp.float32)).astype(jnp.bfloat16)


def three_pass(left, right, dims=CONTRACT_PLAIN):
    first, second = halves_of(left)
    third, fourth = halves_of(right)

    def dot(one, two):
        return lax.dot_general(one, two, dims, preferred_element_type=jnp.float32)

    return dot(first, third) + (dot(first, fourth) + dot(second, third))


def thirds(value):
    first = value.astype(jnp.bfloat16)
    rest = value - first.astype(jnp.float32)
    second = rest.astype(jnp.bfloat16)
    third = (rest - second.astype(jnp.float32)).astype(jnp.bfloat16)
    return first, second, third


def exact_left(value, gradient, dims):
    total = None
    for term in reversed(thirds(value)):
        product = lax.dot_general(term, gradient, dims, preferred_element_type=jnp.float32)
        total = product if total is None else total + product
    return total


def exact_right(gradient, value, dims):
    total = None
    for term in reversed(thirds(value)):
        product = lax.dot_general(gradient, term, dims, preferred_element_type=jnp.float32)
        total = product if total is None else total + product
    return total


def adam_moments(gradient, mean_now, power_now):
    mean_next = decay_first * mean_now + (1.0 - decay_first) * gradient
    power_next = decay_second * power_now + (1.0 - decay_second) * gradient * gradient
    fix_first = 1.0 - decay_first**STEP
    fix_second = 1.0 - decay_second**STEP
    normed = mean_next / fix_first / (jnp.sqrt(power_next / fix_second) + adam_epsilon)
    return (normed, mean_next, power_next)


def square_sum(value):
    return jnp.sum(jnp.sum(value * value, axis=1, keepdims=True), axis=0, keepdims=True)


def project_kernel(core, *refs):
    count = 7
    sources = refs[:count]
    keep, send, whole = refs[count : count + 3]
    held = refs[count + 3 : count + 3 + count]
    done = refs[-1]
    copies = [
        pltpu.make_async_copy(source, target, done.at[index])
        for index, (source, target) in enumerate(zip(sources, held))
    ]
    for copy in copies:
        copy.start()
    ag, ug, dg_t, ab, ub, db, vg = held
    heads = ag.shape[0]
    for index in (0, 3):
        copies[index].wait()
    parts = []
    squares = jnp.zeros((1, 1), jnp.float32)
    for m in range(heads):
        gradient = ag[m]
        parts.append(exact_left(ab[m], gradient, CONTRACT_FIRST))
        squares = squares + square_sum(gradient.astype(jnp.float32))
    for index in (1, 4):
        copies[index].wait()
    gradient = ug[...]
    parts.append(exact_left(ub[...], gradient, CONTRACT_FIRST))
    squares = squares + square_sum(gradient.astype(jnp.float32))
    for index in (2, 5, 6):
        copies[index].wait()
    gradient = dg_t[...]
    parts.append(exact_left(db[...], gradient, CONTRACT_MIXED))
    squares = squares + square_sum(gradient.astype(jnp.float32)) + square_sum(vg[...])
    column = sum(part.shape[1] for part in parts)
    parts.append(jnp.broadcast_to(squares, (whole.shape[0], whole.shape[1] - column)))
    whole[...] = jnp.concatenate(parts, axis=1)
    block = keep.shape[1]
    mine = core[0]
    for row in range(keep.shape[0]):
        keep[row] = whole[pl.ds(pl.multiple_of((2 * row + mine) * block, block), block), :]
        send[row] = whole[pl.ds(pl.multiple_of((2 * row + 1 - mine) * block, block), block), :]


def widen_kernel(ag, ug, dg_t, wide):
    heads, rows, width = ag.shape
    parts = [ag[m].astype(jnp.float32) for m in range(heads)] + [ug[...].astype(jnp.float32)]
    wide[:rows, :] = jnp.concatenate(parts, axis=1)
    lower = dg_t[...].astype(jnp.float32)
    for k in range(lower.shape[0] // rows):
        start = k * lower.shape[1]
        wide[rows:, start : start + lower.shape[1]] = lower[k * rows : (k + 1) * rows, :]


def sum_kernel(column, parts, squares, total, copies):
    value = parts[0]
    for row in range(1, parts.shape[0]):
        value = value + parts[row]
    lanes = lax.broadcasted_iota(jnp.int32, value.shape, 1)
    value = jnp.where(lanes < column, value, squares[0:1, 0:1])
    total[...] = value
    for row in range(copies.shape[0]):
        copies[row] = value


def moments_kernel(
    factor, sums, am, ap, um, up, dm, dp, vg, vm, vp,
    normed, am_out, ap_out, um_out, up_out, dm_out, dp_out, vs_out, vm_out, vp_out,
):
    scale = factor[0:1, 0:1]
    heads = am.shape[0]
    width = am.shape[2]
    column = 0
    parts = []
    value = sums[...] * scale
    for m in range(heads):
        step, mean, power = adam_moments(value[:, column : column + width], am[m], ap[m])
        parts.append(step)
        am_out[m] = mean
        ap_out[m] = power
        column += width
    for mean_now, power_now, mean_out, power_out in (
        (um, up, um_out, up_out), (dm, dp, dm_out, dp_out)
    ):
        width = mean_now.shape[1]
        step, mean, power = adam_moments(
            value[:, column : column + width], mean_now[...], power_now[...]
        )
        parts.append(step)
        mean_out[...] = mean
        power_out[...] = power
        column += width
    parts.append(jnp.zeros((value.shape[0], value.shape[1] - column), jnp.float32))
    normed[...] = jnp.concatenate(parts, axis=1)
    step, mean, power = adam_moments(vg[...] * scale, vm[...], vp[...])
    vs_out[...] = step
    vm_out[...] = mean
    vp_out[...] = power


def subspace_kernel(core, halves, ag, ug, dg_t, wide, pieces, squares):
    mine = core[0]
    value = jnp.concatenate([halves[row] for row in range(halves.shape[0])], axis=0)
    heads, rows, width = ag.shape
    there = wide[...].astype(jnp.bfloat16)
    tall = dg_t.shape[1]
    both = [
        jnp.concatenate([ag[m], there[:rows, m * width : (m + 1) * width]], axis=0)
        for m in range(heads)
    ]
    both.append(jnp.concatenate([ug[...], there[:rows, heads * width :]], axis=0))
    lower = [there[rows:, k * tall : (k + 1) * tall] for k in range(dg_t.shape[0] // rows)]
    both.append(jnp.concatenate([dg_t[...], jnp.concatenate(lower, axis=0)], axis=1))
    places = [pl.multiple_of(place * PIECE, PIECE) for place in (mine, 1 - mine)]
    slot = 0
    column = 0
    for index, gradient in enumerate(both):
        dims = CONTRACT_MIXED if index == heads + 1 else CONTRACT_LAST
        columns = gradient.shape[0] if index == heads + 1 else gradient.shape[1]
        product = exact_right(gradient, value[:, column : column + columns], dims)
        column += columns
        size = product.shape[0] // 2
        for start in range(0, size, PIECE):
            stop = min(size, start + PIECE)
            for k, place in enumerate(places):
                part = product[k * size + start : k * size + stop]
                if stop - start < PIECE:
                    gap = jnp.zeros((PIECE - stop + start, product.shape[1]), jnp.float32)
                    part = jnp.concatenate([part, gap], axis=0)
                pieces[slot, pl.ds(place, PIECE), :] = part
            slot += 1
    total = halves[0][0:1, column : column + 1]
    for row in range(1, halves.shape[0]):
        total = total + halves[row][0:1, column : column + 1]
    squares[...] = jnp.broadcast_to(total, squares.shape)


def gram_kernel(parts, rows_out, packed):
    tensors = parts.shape[0] // 2
    halves = []
    for core in range(2):
        value = parts[core]
        for t in range(1, tensors):
            value = value + parts[2 * t + core]
        halves.append(value)
    rows = jnp.concatenate(halves, axis=1)
    rows_out[...] = rows
    gram = highest(rows, rows, CONTRACT_FIRST)
    half = gram.shape[0] // 2
    quarter = half // 2
    packed[:half, :] = gram[:half, :]
    packed[half:, :half] = gram[half : half + quarter, half:]
    packed[half:, half:] = gram[half + quarter :, half:]


def spread_kernel(first, second, third, copies):
    value = first[...] + (second[...] + third[...])
    for row in range(copies.shape[0]):
        copies[row] = value


def refine_kernel(limit, members, packs, rows, squares, pieces, factor_out):
    pack = packs[0]
    for row in range(1, packs.shape[0]):
        pack = pack + packs[row]
    half = pack.shape[1] // 2
    top = pack[:half, :]
    corner = jnp.concatenate([pack[half:, :half], pack[half:, half:]], axis=0)
    factor = limit / jnp.maximum(jnp.sqrt(squares[0:1, 0:1]), limit)
    factor_out[...] = jnp.broadcast_to(factor, factor_out.shape)
    gram = jnp.concatenate(
        [top, jnp.concatenate([top[:, half:].T, corner], axis=1)], axis=0
    )
    size = gram.shape[0]
    identity = (
        lax.broadcasted_iota(jnp.int32, (size, size), 0)
        == lax.broadcasted_iota(jnp.int32, (size, size), 1)
    ).astype(jnp.float32)
    trace = jnp.sum(jnp.sum(gram * identity, axis=1, keepdims=True), axis=0, keepdims=True)
    squared = factor * factor
    scale = squared / (squared * jnp.sqrt(trace) + norm_epsilon)
    frame = rows[...] * scale
    gram = gram * (scale * scale)
    for sweep in range(NS_STEPS):
        square = three_pass(gram, gram)
        poly = quintic_one * identity + quintic_two * gram + quintic_three * square
        if sweep + 1 < NS_STEPS:
            frame = three_pass(frame, poly)
            gram = three_pass(poly, three_pass(gram, poly))
    block = size // (2 * members)
    order = [c * members + y for y in range(members) for c in range(2)]
    poly = jnp.concatenate([poly[:, k * block : (k + 1) * block] for k in order], axis=1)
    frame = three_pass(frame, poly)
    for t in range(pieces.shape[0] // 2):
        for core in range(2):
            pieces[2 * t + core] = frame[core * PIECE : (core + 1) * PIECE, :]


def frames_kernel(pieces, attention, up, down):
    for m in range(attention.shape[0]):
        attention[m] = pieces[m, : attention.shape[1], :]
    slot = attention.shape[0]
    up[...] = pieces[slot, : up.shape[0], :]
    for k in range(down.shape[0] // PIECE):
        down[k * PIECE : (k + 1) * PIECE, :] = pieces[slot + 1 + k]


def update_kernel(where, *refs):
    ab, ub, db, step_attention, step_up, step_down_t, whole = refs[-7:]
    count = (len(refs) - 7) // 2
    own, other = refs[:count], refs[count : 2 * count]
    block = own[0].shape[0]
    mine = where[0]
    for shift in range(count):
        row = 2 * lax.rem(where[1] + (count - shift), count)
        whole[pl.ds(pl.multiple_of((row + mine) * block, block), block), :] = own[shift][...]
        whole[pl.ds(pl.multiple_of((row + 1 - mine) * block, block), block), :] = other[shift][...]
    value = whole[...]
    column = 0
    heads = ab.shape[0]
    width = step_attention.shape[2]
    for m in range(heads):
        step_attention[m] = galore_scale * three_pass(ab[m], value[:, column : column + width])
        column += width
    width = step_up.shape[1]
    step_up[...] = galore_scale * three_pass(ub[...], value[:, column : column + width])
    column += width
    width = step_down_t.shape[0]
    part = value[:, column : column + width]
    step_down_t[...] = galore_scale * three_pass(part, db[...], CONTRACT_MIXED)


def shape_of(*shape):
    return jax.ShapeDtypeStruct(shape, jnp.float32)


def call(kernel, operands, outs, scratch=(), scalar=False, fetch=False, after=()):
    single = not isinstance(outs, (tuple, list))
    out_list = [outs] if single else list(outs)
    moved = sum(4 * math.prod(o.shape) for o in out_list)
    moved += sum(o.dtype.itemsize * o.size for o in operands)
    specs = [HBM if fetch else VMEM] * len(operands)
    if scalar:
        specs[0] = SMEM
    count = len(operands)
    operands = (*operands, *after)
    specs = specs + [pl.BlockSpec(memory_space=pl.ANY)] * len(after)

    def body(*refs):
        kernel(*refs[:count], *refs[count + len(after) :])

    return pl.pallas_call(
        body,
        out_shape=outs,
        in_specs=specs,
        out_specs=VMEM if single else [VMEM] * len(out_list),
        scratch_shapes=list(scratch),
        compiler_params=pltpu.CompilerParams(vmem_limit_bytes=(60 if fetch else 32) << 20),
        cost_estimate=pl.CostEstimate(flops=0, bytes_accessed=moved, transcendentals=0),
    )(*operands)


def sum_over(value, axis, masks):
    total = value
    for mask in masks:
        pairs = [(k, k ^ mask) for k in range(lax.axis_size(axis))]
        total = total + lax.ppermute(value, axis, pairs)
    return total


def exchange(value, axes):
    return lax.all_to_all(value, axes, split_axis=0, concat_axis=0, tiled=True)


def on_device(ag, ug, dg, ab, ub, db, am, ap, um, up, dm, dp, vg, vm, vp):
    heads, rows, width = ag.shape
    rank = ab.shape[2]
    block = am.shape[1]
    columns = heads * width + ug.shape[1] + dg.shape[1]
    padded = -(-(columns + 1) // 128) * 128
    tensors = lax.axis_size("x")
    planes = lax.axis_size("z")
    members = lax.axis_size("y")
    owners = tensors * lax.axis_size("c")
    entries = (ag.size + ug.size + dg.size + vg.size) * planes * members * owners
    limit = float(clip_rms * math.sqrt(entries))
    where = jnp.stack([lax.axis_index("c"), lax.axis_index("y")]).astype(jnp.int32)
    f32 = jnp.float32

    dg_t = dg.T
    first_operands = (ag, ug, dg_t, ab, ub, db, vg)
    keep, send = call(
        project_kernel,
        (where, *first_operands),
        (shape_of(members, block, padded), shape_of(members, block, padded)),
        scratch=[pltpu.VMEM((rank, padded), f32)]
        + [pltpu.VMEM(o.shape, o.dtype) for o in first_operands]
        + [pltpu.SemaphoreType.DMA((len(first_operands),))],
        scalar=True,
        fetch=True,
    )
    swap = [(0, 1), (1, 0)]

    chip = keep + lax.ppermute(send, "c", swap)
    squares = jnp.broadcast_to(chip[0, :8, columns : columns + 1], (8, 128))
    scattered = exchange(chip, "y")
    wide = call(
        widen_kernel,
        (ag, ug, dg_t),
        shape_of(2 * rows, heads * width + ug.shape[1]),
        after=(squares,),
    )
    wide = lax.ppermute(wide, "c", swap)
    near = [k for k in range(1, min(4, planes))]
    far = [4 * k for k in range(1, planes // 4)]
    squares = sum_over(squares, "z", near)

    def sum_body(*refs):
        sum_kernel(columns, *refs)

    sums, copies = call(
        sum_body,
        (scattered, squares),
        (shape_of(block, padded), shape_of(members, block, padded)),
        after=(wide,),
    )
    own = exchange(copies, "y")
    pieces, squares = call(
        subspace_kernel,
        (where, own, ag, ug, dg_t, wide),
        (shape_of(owners, 2 * PIECE, rank // 2), shape_of(8, 128)),
        scalar=True,
    )
    squares = sum_over(squares, "z", far)
    parts = exchange(pieces, OWNERS)
    packed_rows = 3 * rank // 4
    own_rows, packed = call(
        gram_kernel,
        (parts,),
        (shape_of(2 * PIECE, rank), shape_of(packed_rows, rank)),
        after=(squares,),
    )
    squares = sum_over(squares, "x", range(1, tensors))
    first = owners - 3
    places = [(s % 2) * tensors + s // 2 for s in range(first, owners)]
    ring = [(places[k], places[(k + 1) % 3]) for k in range(3)]
    back = [(b, a) for a, b in ring]
    second = lax.ppermute(packed, ("c", "x"), ring)
    third = lax.ppermute(packed, ("c", "x"), back)
    grams = call(spread_kernel, (packed, second, third), shape_of(members, packed_rows, rank))
    grams = exchange(grams, "y")

    def refine_body(*refs):
        refine_kernel(limit, members, *refs)

    frames, factor = call(
        refine_body,
        (grams, own_rows, squares),
        (shape_of(owners, PIECE, rank), shape_of(8, 128)),
    )
    frames = exchange(frames, OWNERS)
    normed, am2, ap2, um2, up2, dm2, dp2, vs2, vm2, vp2 = call(
        moments_kernel,
        (factor, sums, am, ap, um, up, dm, dp, vg, vm, vp),
        [shape_of(block, padded)]
        + [shape_of(*v.shape) for v in (am, ap, um, up, dm, dp, vg, vm, vp)],
    )
    own_normed = [normed]
    for shift in range(1, members):
        pairs = [(k, (k + shift) % members) for k in range(members)]
        own_normed.append(lax.ppermute(normed, "y", pairs))
    other_normed = [lax.ppermute(value, "c", swap) for value in own_normed]
    step_attention, step_up, step_down_t = call(
        update_kernel,
        (where, *own_normed, *other_normed, ab, ub, db),
        [shape_of(*v.shape) for v in (ag, ug, dg_t)],
        scratch=[pltpu.VMEM((rank, padded), f32)],
        scalar=True,
    )
    basis_attention, basis_up, basis_down = call(
        frames_kernel, (frames,), [shape_of(*v.shape) for v in (ab, ub, db)]
    )
    return (
        step_attention, step_up, step_down_t.T,
        am2, ap2, um2, up2, dm2, dp2,
        basis_attention, basis_up, basis_down,
        vs2, vm2, vp2,
    )


def solution(mesh):
    tensors = mesh.shape["tensor"]
    split = Mesh(mesh.devices.reshape(-1, 4, 2, tensors), SHARD_TENSOR)
    stacked = P(None, SHARD, "x")
    flat = P(SHARD, "x")
    vector = P(None, SHARD_TENSOR)
    bases = (P(None, SHARD, None), P(SHARD, None), P(SHARD, None))
    moments = (stacked, stacked, flat, flat, flat, flat)
    in_specs = (stacked, flat, flat) + bases + moments + (vector,) * 3
    out_specs = (stacked, flat, flat) + moments + bases + (vector,) * 3
    return jax.shard_map(
        on_device, mesh=split, in_specs=in_specs, out_specs=out_specs, check_vma=False
    )
```

```python
import math

import jax
import jax.numpy as jnp
from jax import lax
from jax.experimental import pallas as pl
from jax.experimental.pallas import tpu as pltpu
from jax.sharding import Mesh
from jax.sharding import PartitionSpec as P

NS_STEPS = 3
STEP = 10
SHARD = ("z", "y", "c")
SHARD_TENSOR = ("z", "y", "c", "x")
OWNERS = ("x", "c")
PIECE = 128
EXTRA = 8
VMEM = pl.BlockSpec(memory_space=pltpu.VMEM)
HBM = pl.BlockSpec(memory_space=pltpu.HBM)
SMEM = pl.BlockSpec(memory_space=pltpu.SMEM)

quintic_one = 3.4445
quintic_two = -4.775
quintic_three = 2.0315
decay_first = 0.9
decay_second = 0.95
adam_epsilon = 1e-08
norm_epsilon = 1e-07
galore_scale = 0.25
clip_rms = 1.0

CONTRACT_FIRST = (((0,), (0,)), ((), ()))
CONTRACT_LAST = (((1,), (1,)), ((), ()))
CONTRACT_MIXED = (((0,), (1,)), ((), ()))
CONTRACT_PLAIN = (((1,), (0,)), ((), ()))


def highest(left, right, dims=CONTRACT_PLAIN):
    return lax.dot_general(
        left, right, dims, precision=lax.Precision.HIGHEST, preferred_element_type=jnp.float32
    )


def halves_of(value):
    first = value.astype(jnp.bfloat16)
    return first, (value - first.astype(jnp.float32)).astype(jnp.bfloat16)


def three_pass(left, right, dims=CONTRACT_PLAIN):
    first, second = halves_of(left)
    third, fourth = halves_of(right)

    def dot(one, two):
        return lax.dot_general(one, two, dims, preferred_element_type=jnp.float32)

    return dot(first, third) + (dot(first, fourth) + dot(second, third))


def thirds(value):
    first = value.astype(jnp.bfloat16)
    rest = value - first.astype(jnp.float32)
    second = rest.astype(jnp.bfloat16)
    third = (rest - second.astype(jnp.float32)).astype(jnp.bfloat16)
    return first, second, third


def exact_left(value, gradient, dims):
    total = None
    for term in reversed(thirds(value)):
        product = lax.dot_general(term, gradient, dims, preferred_element_type=jnp.float32)
        total = product if total is None else total + product
    return total


def exact_right(gradient, value, dims):
    total = None
    for term in reversed(thirds(value)):
        product = lax.dot_general(gradient, term, dims, preferred_element_type=jnp.float32)
        total = product if total is None else total + product
    return total


def adam_moments(gradient, mean_now, power_now):
    mean_next = decay_first * mean_now + (1.0 - decay_first) * gradient
    power_next = decay_second * power_now + (1.0 - decay_second) * gradient * gradient
    fix_first = 1.0 - decay_first**STEP
    fix_second = 1.0 - decay_second**STEP
    normed = mean_next / fix_first / (jnp.sqrt(power_next / fix_second) + adam_epsilon)
    return (normed, mean_next, power_next)


def square_sum(value):
    return jnp.sum(jnp.sum(value * value, axis=1, keepdims=True), axis=0, keepdims=True)


def project_kernel(core, *refs):
    count = 7
    sources = refs[:count]
    keep, send, whole = refs[count : count + 3]
    held = refs[count + 3 : count + 3 + count]
    done = refs[-1]
    copies = [
        pltpu.make_async_copy(source, target, done.at[index])
        for index, (source, target) in enumerate(zip(sources, held))
    ]
    for copy in copies:
        copy.start()
    ag, ug, dg_t, ab, ub, db, vg = held
    heads = ag.shape[0]
    for index in (0, 3):
        copies[index].wait()
    parts = []
    squares = jnp.zeros((1, 1), jnp.float32)
    for m in range(heads):
        gradient = ag[m]
        parts.append(exact_left(ab[m], gradient, CONTRACT_FIRST))
        squares = squares + square_sum(gradient.astype(jnp.float32))
    for index in (1, 4):
        copies[index].wait()
    gradient = ug[...]
    parts.append(exact_left(ub[...], gradient, CONTRACT_FIRST))
    squares = squares + square_sum(gradient.astype(jnp.float32))
    for index in (2, 5, 6):
        copies[index].wait()
    gradient = dg_t[...]
    parts.append(exact_left(db[...], gradient, CONTRACT_MIXED))
    squares = squares + square_sum(gradient.astype(jnp.float32)) + square_sum(vg[...])
    column = sum(part.shape[1] for part in parts)
    parts.append(jnp.broadcast_to(squares, (whole.shape[0], whole.shape[1] - column)))
    whole[...] = jnp.concatenate(parts, axis=1)
    block = keep.shape[1]
    mine = core[0]
    for row in range(keep.shape[0]):
        keep[row] = whole[pl.ds(pl.multiple_of((2 * row + mine) * block, block), block), :]
        send[row] = whole[pl.ds(pl.multiple_of((2 * row + 1 - mine) * block, block), block), :]


def widen_kernel(ag, ug, dg_t, wide):
    heads, rows, width = ag.shape
    parts = [ag[m].astype(jnp.float32) for m in range(heads)] + [ug[...].astype(jnp.float32)]
    wide[:rows, :] = jnp.concatenate(parts, axis=1)
    lower = dg_t[...].astype(jnp.float32)
    for k in range(lower.shape[0] // rows):
        start = k * lower.shape[1]
        wide[rows:, start : start + lower.shape[1]] = lower[k * rows : (k + 1) * rows, :]


def chip_kernel(column, keep, received, chip, squares):
    value = keep[...] + received[...]
    chip[...] = value
    squares[...] = jnp.broadcast_to(value[0, 0:1, column : column + 1], squares.shape)


def chip_sum(column, keep, received):
    count, block, padded = keep.shape
    spec = pl.BlockSpec((1, block, padded), lambda i: (i, 0, 0))

    def body(*refs):
        chip_kernel(column, *refs)

    return pl.pallas_call(
        body,
        out_shape=(shape_of(*keep.shape), shape_of(8, 128)),
        grid=(count,),
        in_specs=[spec, spec],
        out_specs=[spec, pl.BlockSpec((8, 128), lambda i: (0, 0))],
        compiler_params=pltpu.CompilerParams(vmem_limit_bytes=16 << 20),
        cost_estimate=pl.CostEstimate(
            flops=0, bytes_accessed=12 * keep.size, transcendentals=0
        ),
    )(keep, received)


def sum_kernel(parts, total, copies):
    value = parts[0]
    for row in range(1, parts.shape[0]):
        value = value + parts[row]
    total[...] = value
    for row in range(copies.shape[0]):
        copies[row] = value


def moments_kernel(
    factor, sums, am, ap, um, up, dm, dp, vg, vm, vp,
    normed, am_out, ap_out, um_out, up_out, dm_out, dp_out, vs_out, vm_out, vp_out,
):
    scale = factor[0:1, 0:1]
    heads = am.shape[0]
    width = am.shape[2]
    column = 0
    parts = []
    value = sums[...] * scale
    for m in range(heads):
        step, mean, power = adam_moments(value[:, column : column + width], am[m], ap[m])
        parts.append(step)
        am_out[m] = mean
        ap_out[m] = power
        column += width
    for mean_now, power_now, mean_out, power_out in (
        (um, up, um_out, up_out), (dm, dp, dm_out, dp_out)
    ):
        width = mean_now.shape[1]
        step, mean, power = adam_moments(
            value[:, column : column + width], mean_now[...], power_now[...]
        )
        parts.append(step)
        mean_out[...] = mean
        power_out[...] = power
        column += width
    parts.append(jnp.zeros((value.shape[0], value.shape[1] - column), jnp.float32))
    normed[...] = jnp.concatenate(parts, axis=1)
    step, mean, power = adam_moments(vg[...] * scale, vm[...], vp[...])
    vs_out[...] = step
    vm_out[...] = mean
    vp_out[...] = power


def subspace_kernel(core, halves, ag, ug, dg_t, wide, pieces):
    mine = core[0]
    value = jnp.concatenate([halves[row] for row in range(halves.shape[0])], axis=0)
    heads, rows, width = ag.shape
    there = wide[...].astype(jnp.bfloat16)
    tall = dg_t.shape[1]
    both = [
        jnp.concatenate([ag[m], there[:rows, m * width : (m + 1) * width]], axis=0)
        for m in range(heads)
    ]
    both.append(jnp.concatenate([ug[...], there[:rows, heads * width :]], axis=0))
    lower = [there[rows:, k * tall : (k + 1) * tall] for k in range(dg_t.shape[0] // rows)]
    both.append(jnp.concatenate([dg_t[...], jnp.concatenate(lower, axis=0)], axis=1))
    places = [pl.multiple_of(place * PIECE, PIECE) for place in (mine, 1 - mine)]
    slot = 0
    column = 0
    for index, gradient in enumerate(both):
        dims = CONTRACT_MIXED if index == heads + 1 else CONTRACT_LAST
        columns = gradient.shape[0] if index == heads + 1 else gradient.shape[1]
        product = exact_right(gradient, value[:, column : column + columns], dims)
        column += columns
        size = product.shape[0] // 2
        for start in range(0, size, PIECE):
            stop = min(size, start + PIECE)
            for k, place in enumerate(places):
                part = product[k * size + start : k * size + stop]
                if stop - start < PIECE:
                    gap = jnp.zeros((PIECE - stop + start, product.shape[1]), jnp.float32)
                    part = jnp.concatenate([part, gap], axis=0)
                pieces[slot, pl.ds(place, PIECE), :] = part
            slot += 1


def gram_kernel(parts, squares, rows_out, packed):
    tensors = parts.shape[0] // 2
    halves = []
    for core in range(2):
        value = parts[core]
        for t in range(1, tensors):
            value = value + parts[2 * t + core]
        halves.append(value)
    rows = jnp.concatenate(halves, axis=1)
    rows_out[...] = rows
    gram = highest(rows, rows, CONTRACT_FIRST)
    half = gram.shape[0] // 2
    last = half + half // 2
    packed[:half, :] = gram[:half, :]
    packed[half:last, :half] = gram[half:last, half:]
    packed[half:last, half:] = gram[last:, half:]
    packed[last:, :] = jnp.broadcast_to(squares[0:1, 0:1], (EXTRA, packed.shape[1]))


def spread_kernel(first, second, third, copies):
    size = first.shape[0] - EXTRA
    value = first[:size, :] + (second[:size, :] + third[:size, :])
    for row in range(copies.shape[0]):
        copies[row, :size, :] = value
        copies[row, size:, :] = first[size:, :]


def refine_kernel(limit, members, packs, rows, pieces, factor_out):
    pack = packs[0]
    for row in range(1, packs.shape[0]):
        pack = pack + packs[row]
    half = pack.shape[1] // 2
    last = pack.shape[0] - EXTRA
    top = pack[:half, :]
    corner = jnp.concatenate([pack[half:last, :half], pack[half:last, half:]], axis=0)
    factor = limit / jnp.maximum(jnp.sqrt(pack[last : last + 1, 0:1]), limit)
    factor_out[...] = jnp.broadcast_to(factor, factor_out.shape)
    gram = jnp.concatenate(
        [top, jnp.concatenate([top[:, half:].T, corner], axis=1)], axis=0
    )
    size = gram.shape[0]
    identity = (
        lax.broadcasted_iota(jnp.int32, (size, size), 0)
        == lax.broadcasted_iota(jnp.int32, (size, size), 1)
    ).astype(jnp.float32)
    trace = jnp.sum(jnp.sum(gram * identity, axis=1, keepdims=True), axis=0, keepdims=True)
    squared = factor * factor
    scale = squared / (squared * jnp.sqrt(trace) + norm_epsilon)
    frame = rows[...] * scale
    gram = gram * (scale * scale)
    for sweep in range(NS_STEPS):
        square = three_pass(gram, gram)
        poly = quintic_one * identity + quintic_two * gram + quintic_three * square
        if sweep + 1 < NS_STEPS:
            frame = three_pass(frame, poly)
            gram = three_pass(poly, three_pass(gram, poly))
    block = size // (2 * members)
    order = [c * members + y for y in range(members) for c in range(2)]
    poly = jnp.concatenate([poly[:, k * block : (k + 1) * block] for k in order], axis=1)
    frame = three_pass(frame, poly)
    for t in range(pieces.shape[0] // 2):
        for core in range(2):
            pieces[2 * t + core] = frame[core * PIECE : (core + 1) * PIECE, :]


def frames_kernel(pieces, attention, up, down):
    for m in range(attention.shape[0]):
        attention[m] = pieces[m, : attention.shape[1], :]
    slot = attention.shape[0]
    up[...] = pieces[slot, : up.shape[0], :]
    for k in range(down.shape[0] // PIECE):
        down[k * PIECE : (k + 1) * PIECE, :] = pieces[slot + 1 + k]


def update_kernel(core, line, *refs):
    ab, ub, db, step_attention, step_up, step_down_t, whole = refs[-7:]
    count = (len(refs) - 7) // 2
    own, other = refs[:count], refs[count : 2 * count]
    block = own[0].shape[0]
    mine = core[0]
    for shift in range(count):
        row = 2 * lax.rem(line[0] + (count - shift), count)
        whole[pl.ds(pl.multiple_of((row + mine) * block, block), block), :] = own[shift][...]
        whole[pl.ds(pl.multiple_of((row + 1 - mine) * block, block), block), :] = other[shift][...]
    value = whole[...]
    column = 0
    heads = ab.shape[0]
    width = step_attention.shape[2]
    for m in range(heads):
        step_attention[m] = galore_scale * three_pass(ab[m], value[:, column : column + width])
        column += width
    width = step_up.shape[1]
    step_up[...] = galore_scale * three_pass(ub[...], value[:, column : column + width])
    column += width
    width = step_down_t.shape[0]
    part = value[:, column : column + width]
    step_down_t[...] = galore_scale * three_pass(part, db[...], CONTRACT_MIXED)


def shape_of(*shape):
    return jax.ShapeDtypeStruct(shape, jnp.float32)


def call(kernel, operands, outs, scratch=(), scalars=0, fetch=False, after=()):
    single = not isinstance(outs, (tuple, list))
    out_list = [outs] if single else list(outs)
    moved = sum(4 * math.prod(o.shape) for o in out_list)
    moved += sum(o.dtype.itemsize * o.size for o in operands)
    specs = [HBM if fetch else VMEM] * len(operands)
    specs[:scalars] = [SMEM] * scalars
    count = len(operands)
    operands = (*operands, *after)
    specs = specs + [pl.BlockSpec(memory_space=pl.ANY)] * len(after)

    def body(*refs):
        kernel(*refs[:count], *refs[count + len(after) :])

    return pl.pallas_call(
        body,
        out_shape=outs,
        in_specs=specs,
        out_specs=VMEM if single else [VMEM] * len(out_list),
        scratch_shapes=list(scratch),
        compiler_params=pltpu.CompilerParams(vmem_limit_bytes=(60 if fetch else 32) << 20),
        cost_estimate=pl.CostEstimate(flops=0, bytes_accessed=moved, transcendentals=0),
    )(*operands)


def sum_over(value, axis, masks):
    total = value
    for mask in masks:
        pairs = [(k, k ^ mask) for k in range(lax.axis_size(axis))]
        total = total + lax.ppermute(value, axis, pairs)
    return total


def exchange(value, axes):
    return lax.all_to_all(value, axes, split_axis=0, concat_axis=0, tiled=True)


def on_device(ag, ug, dg, ab, ub, db, am, ap, um, up, dm, dp, vg, vm, vp):
    heads, rows, width = ag.shape
    rank = ab.shape[2]
    block = am.shape[1]
    columns = heads * width + ug.shape[1] + dg.shape[1]
    padded = -(-(columns + 1) // 128) * 128
    tensors = lax.axis_size("x")
    planes = lax.axis_size("z")
    members = lax.axis_size("y")
    owners = tensors * lax.axis_size("c")
    entries = (ag.size + ug.size + dg.size + vg.size) * planes * members * owners
    limit = float(clip_rms * math.sqrt(entries))
    core = lax.axis_index("c").astype(jnp.int32).reshape(1)
    line = lax.axis_index("y").astype(jnp.int32).reshape(1)
    f32 = jnp.float32

    dg_t = dg.T
    first_operands = (ag, ug, dg_t, ab, ub, db, vg)
    keep, send = call(
        project_kernel,
        (core, *first_operands),
        (shape_of(members, block, padded), shape_of(members, block, padded)),
        scratch=[pltpu.VMEM((rank, padded), f32)]
        + [pltpu.VMEM(o.shape, o.dtype) for o in first_operands]
        + [pltpu.SemaphoreType.DMA((len(first_operands),))],
        scalars=1,
        fetch=True,
    )
    swap = [(0, 1), (1, 0)]

    send = lax.ppermute(send, "c", swap)
    wide = call(
        widen_kernel,
        (ag, ug, dg_t),
        shape_of(2 * rows, heads * width + ug.shape[1]),
        after=(keep,),
    )
    wide = lax.ppermute(wide, "c", swap)
    chip, squares = chip_sum(columns, keep, send)
    scattered = exchange(chip, "y")
    near = [k for k in range(1, min(4, planes))]
    far = [1 << k for k in range(2, planes.bit_length() - 1)]
    squares = sum_over(squares, "z", near)
    sums, copies = call(
        sum_kernel,
        (scattered,),
        (shape_of(block, padded), shape_of(members, block, padded)),
        after=(squares, wide),
    )
    own = exchange(copies, "y")
    squares = sum_over(squares, "x", range(1, tensors))
    pieces = call(
        subspace_kernel,
        (core, own, ag, ug, dg_t, wide),
        shape_of(owners, 2 * PIECE, rank // 2),
        scalars=1,
        after=(squares,),
    )
    for mask in reversed(far):
        squares = sum_over(squares, "z", [mask])
    parts = exchange(pieces, OWNERS)
    packed_rows = 3 * rank // 4 + EXTRA
    own_rows, packed = call(
        gram_kernel,
        (parts, squares),
        (shape_of(2 * PIECE, rank), shape_of(packed_rows, rank)),
    )
    first = owners - 3
    places = [(s % 2) * tensors + s // 2 for s in range(first, owners)]
    ring = [(places[k], places[(k + 1) % 3]) for k in range(3)]
    back = [(b, a) for a, b in ring]
    second = lax.ppermute(packed, ("c", "x"), ring)
    third = lax.ppermute(packed, ("c", "x"), back)
    grams = call(spread_kernel, (packed, second, third), shape_of(members, packed_rows, rank))
    grams = exchange(grams, "y")

    def refine_body(*refs):
        refine_kernel(limit, members, *refs)

    frames, factor = call(
        refine_body,
        (grams, own_rows),
        (shape_of(owners, PIECE, rank), shape_of(8, 128)),
    )
    frames = exchange(frames, OWNERS)
    normed, am2, ap2, um2, up2, dm2, dp2, vs2, vm2, vp2 = call(
        moments_kernel,
        (factor, sums, am, ap, um, up, dm, dp, vg, vm, vp),
        [shape_of(block, padded)]
        + [shape_of(*v.shape) for v in (am, ap, um, up, dm, dp, vg, vm, vp)],
    )
    own_normed = [normed]
    for shift in range(1, members):
        pairs = [(k, (k + shift) % members) for k in range(members)]
        own_normed.append(lax.ppermute(normed, "y", pairs))
    other_normed = [lax.ppermute(value, "c", swap) for value in own_normed]
    step_attention, step_up, step_down_t = call(
        update_kernel,
        (core, line, *own_normed, *other_normed, ab, ub, db),
        [shape_of(*v.shape) for v in (ag, ug, dg_t)],
        scratch=[pltpu.VMEM((rank, padded), f32)],
        scalars=2,
    )
    basis_attention, basis_up, basis_down = call(
        frames_kernel,
        (frames,),
        [shape_of(*v.shape) for v in (ab, ub, db)],
    )
    return (
        step_attention, step_up, step_down_t.T,
        am2, ap2, um2, up2, dm2, dp2,
        basis_attention, basis_up, basis_down,
        vs2, vm2, vp2,
    )


def solution(mesh):
    tensors = mesh.shape["tensor"]
    split = Mesh(mesh.devices.reshape(-1, 4, 2, tensors), SHARD_TENSOR)
    stacked = P(None, SHARD, "x")
    flat = P(SHARD, "x")
    vector = P(None, SHARD_TENSOR)
    bases = (P(None, SHARD, None), P(SHARD, None), P(SHARD, None))
    moments = (stacked, stacked, flat, flat, flat, flat)
    in_specs = (stacked, flat, flat) + bases + moments + (vector,) * 3
    out_specs = (stacked, flat, flat) + moments + bases + (vector,) * 3
    return jax.shard_map(
        on_device, mesh=split, in_specs=in_specs, out_specs=out_specs, check_vma=False
    )
```

```python
import math

import jax
import jax.numpy as jnp
from jax import lax
from jax.experimental import pallas as pl
from jax.experimental.pallas import tpu as pltpu
from jax.sharding import Mesh
from jax.sharding import PartitionSpec as P

NS_STEPS = 3
STEP = 10
SHARD = ("z", "y", "c")
SHARD_TENSOR = ("z", "y", "c", "x")
OWNERS = ("x", "c")
PIECE = 128
EXTRA = 8
VMEM = pl.BlockSpec(memory_space=pltpu.VMEM)
HBM = pl.BlockSpec(memory_space=pltpu.HBM)
SMEM = pl.BlockSpec(memory_space=pltpu.SMEM)

quintic_one = 3.4445
quintic_two = -4.775
quintic_three = 2.0315
decay_first = 0.9
decay_second = 0.95
adam_epsilon = 1e-08
norm_epsilon = 1e-07
galore_scale = 0.25
clip_rms = 1.0

CONTRACT_FIRST = (((0,), (0,)), ((), ()))
CONTRACT_LAST = (((1,), (1,)), ((), ()))
CONTRACT_MIXED = (((0,), (1,)), ((), ()))
CONTRACT_PLAIN = (((1,), (0,)), ((), ()))


def highest(left, right, dims=CONTRACT_PLAIN):
    return lax.dot_general(
        left, right, dims, precision=lax.Precision.HIGHEST, preferred_element_type=jnp.float32
    )


def halves_of(value):
    first = value.astype(jnp.bfloat16)
    return first, (value - first.astype(jnp.float32)).astype(jnp.bfloat16)


def three_pass(left, right, dims=CONTRACT_PLAIN):
    first, second = halves_of(left)
    third, fourth = halves_of(right)

    def dot(one, two):
        return lax.dot_general(one, two, dims, preferred_element_type=jnp.float32)

    return dot(first, third) + (dot(first, fourth) + dot(second, third))


def thirds(value):
    first = value.astype(jnp.bfloat16)
    rest = value - first.astype(jnp.float32)
    second = rest.astype(jnp.bfloat16)
    third = (rest - second.astype(jnp.float32)).astype(jnp.bfloat16)
    return first, second, third


def exact_left(value, gradient, dims):
    total = None
    for term in reversed(thirds(value)):
        product = lax.dot_general(term, gradient, dims, preferred_element_type=jnp.float32)
        total = product if total is None else total + product
    return total


def exact_right(gradient, value, dims):
    total = None
    for term in reversed(thirds(value)):
        product = lax.dot_general(gradient, term, dims, preferred_element_type=jnp.float32)
        total = product if total is None else total + product
    return total


def adam_moments(gradient, mean_now, power_now):
    mean_next = decay_first * mean_now + (1.0 - decay_first) * gradient
    power_next = decay_second * power_now + (1.0 - decay_second) * gradient * gradient
    fix_first = 1.0 - decay_first**STEP
    fix_second = 1.0 - decay_second**STEP
    normed = mean_next / fix_first / (jnp.sqrt(power_next / fix_second) + adam_epsilon)
    return (normed, mean_next, power_next)


def square_sum(value):
    return jnp.sum(jnp.sum(value * value, axis=1, keepdims=True), axis=0, keepdims=True)


def project_kernel(core, *refs):
    count = 7
    sources = refs[:count]
    keep, send, wide, whole = refs[count : count + 4]
    held = refs[count + 4 : count + 4 + count]
    done = refs[-1]
    copies = [
        pltpu.make_async_copy(source, target, done.at[index])
        for index, (source, target) in enumerate(zip(sources, held))
    ]
    for copy in copies:
        copy.start()
    ag, ug, dg_t, ab, ub, db, vg = held
    heads = ag.shape[0]
    for index in (0, 3):
        copies[index].wait()
    parts = []
    wides = []
    rows = ug.shape[0]
    squares = jnp.zeros((1, 1), jnp.float32)
    for m in range(heads):
        gradient = ag[m]
        parts.append(exact_left(ab[m], gradient, CONTRACT_FIRST))
        wides.append(gradient.astype(jnp.float32))
        squares = squares + square_sum(wides[-1])
    for index in (1, 4):
        copies[index].wait()
    gradient = ug[...]
    parts.append(exact_left(ub[...], gradient, CONTRACT_FIRST))
    wides.append(gradient.astype(jnp.float32))
    squares = squares + square_sum(wides[-1])
    wide[:rows, :] = jnp.concatenate(wides, axis=1)
    for index in (2, 5, 6):
        copies[index].wait()
    gradient = dg_t[...]
    parts.append(exact_left(db[...], gradient, CONTRACT_MIXED))
    lower = gradient.astype(jnp.float32)
    for k in range(lower.shape[0] // rows):
        start = k * lower.shape[1]
        wide[rows:, start : start + lower.shape[1]] = lower[k * rows : (k + 1) * rows, :]
    squares = squares + square_sum(lower) + square_sum(vg[...])
    column = sum(part.shape[1] for part in parts)
    parts.append(jnp.broadcast_to(squares, (whole.shape[0], whole.shape[1] - column)))
    whole[...] = jnp.concatenate(parts, axis=1)
    block = keep.shape[1]
    mine = core[0]
    for row in range(keep.shape[0]):
        keep[row] = whole[pl.ds(pl.multiple_of((2 * row + mine) * block, block), block), :]
        send[row] = whole[pl.ds(pl.multiple_of((2 * row + 1 - mine) * block, block), block), :]


def chip_kernel(column, keep, received, chip, squares):
    value = keep[...] + received[...]
    chip[...] = value
    squares[...] = jnp.broadcast_to(value[0, 0:1, column : column + 1], squares.shape)


def chip_sum(column, keep, received):
    count, block, padded = keep.shape
    spec = pl.BlockSpec((1, block, padded), lambda i: (i, 0, 0))

    def body(*refs):
        chip_kernel(column, *refs)

    return pl.pallas_call(
        body,
        out_shape=(shape_of(*keep.shape), shape_of(8, 128)),
        grid=(count,),
        in_specs=[spec, spec],
        out_specs=[spec, pl.BlockSpec((8, 128), lambda i: (0, 0))],
        compiler_params=pltpu.CompilerParams(vmem_limit_bytes=16 << 20),
        cost_estimate=pl.CostEstimate(
            flops=0, bytes_accessed=12 * keep.size, transcendentals=0
        ),
    )(keep, received)


def sum_kernel(parts, total, copies):
    value = parts[0]
    for row in range(1, parts.shape[0]):
        value = value + parts[row]
    total[...] = value
    for row in range(copies.shape[0]):
        copies[row] = value


def moments_kernel(
    factor, sums, am, ap, um, up, dm, dp, vg, vm, vp,
    normed, am_out, ap_out, um_out, up_out, dm_out, dp_out, vs_out, vm_out, vp_out,
):
    scale = factor[0:1, 0:1]
    heads = am.shape[0]
    width = am.shape[2]
    column = 0
    parts = []
    value = sums[...] * scale
    for m in range(heads):
        step, mean, power = adam_moments(value[:, column : column + width], am[m], ap[m])
        parts.append(step)
        am_out[m] = mean
        ap_out[m] = power
        column += width
    for mean_now, power_now, mean_out, power_out in (
        (um, up, um_out, up_out), (dm, dp, dm_out, dp_out)
    ):
        width = mean_now.shape[1]
        step, mean, power = adam_moments(
            value[:, column : column + width], mean_now[...], power_now[...]
        )
        parts.append(step)
        mean_out[...] = mean
        power_out[...] = power
        column += width
    parts.append(jnp.zeros((value.shape[0], value.shape[1] - column), jnp.float32))
    normed[...] = jnp.concatenate(parts, axis=1)
    step, mean, power = adam_moments(vg[...] * scale, vm[...], vp[...])
    vs_out[...] = step
    vm_out[...] = mean
    vp_out[...] = power


def subspace_kernel(core, halves, ag, ug, dg_t, wide, pieces):
    mine = core[0]
    value = jnp.concatenate([halves[row] for row in range(halves.shape[0])], axis=0)
    heads, rows, width = ag.shape
    there = wide[...].astype(jnp.bfloat16)
    tall = dg_t.shape[1]
    both = [
        jnp.concatenate([ag[m], there[:rows, m * width : (m + 1) * width]], axis=0)
        for m in range(heads)
    ]
    both.append(jnp.concatenate([ug[...], there[:rows, heads * width :]], axis=0))
    lower = [there[rows:, k * tall : (k + 1) * tall] for k in range(dg_t.shape[0] // rows)]
    both.append(jnp.concatenate([dg_t[...], jnp.concatenate(lower, axis=0)], axis=1))
    places = [pl.multiple_of(place * PIECE, PIECE) for place in (mine, 1 - mine)]
    slot = 0
    column = 0
    for index, gradient in enumerate(both):
        dims = CONTRACT_MIXED if index == heads + 1 else CONTRACT_LAST
        columns = gradient.shape[0] if index == heads + 1 else gradient.shape[1]
        product = exact_right(gradient, value[:, column : column + columns], dims)
        column += columns
        size = product.shape[0] // 2
        for start in range(0, size, PIECE):
            stop = min(size, start + PIECE)
            for k, place in enumerate(places):
                part = product[k * size + start : k * size + stop]
                if stop - start < PIECE:
                    gap = jnp.zeros((PIECE - stop + start, product.shape[1]), jnp.float32)
                    part = jnp.concatenate([part, gap], axis=0)
                pieces[slot, pl.ds(place, PIECE), :] = part
            slot += 1


def gram_kernel(parts, squares, rows_out, packed):
    tensors = parts.shape[0] // 2
    halves = []
    for core in range(2):
        value = parts[core]
        for t in range(1, tensors):
            value = value + parts[2 * t + core]
        halves.append(value)
    rows = jnp.concatenate(halves, axis=1)
    rows_out[...] = rows
    gram = highest(rows, rows, CONTRACT_FIRST)
    half = gram.shape[0] // 2
    last = half + half // 2
    packed[:half, :] = gram[:half, :]
    packed[half:last, :half] = gram[half:last, half:]
    packed[half:last, half:] = gram[last:, half:]
    packed[last:, :] = jnp.broadcast_to(squares[0:1, 0:1], (EXTRA, packed.shape[1]))


def spread_kernel(first, second, third, copies):
    size = first.shape[0] - EXTRA
    value = first[:size, :] + (second[:size, :] + third[:size, :])
    for row in range(copies.shape[0]):
        copies[row, :size, :] = value
        copies[row, size:, :] = first[size:, :]


def refine_kernel(limit, members, packs, rows, pieces, factor_out):
    pack = packs[0]
    for row in range(1, packs.shape[0]):
        pack = pack + packs[row]
    half = pack.shape[1] // 2
    last = pack.shape[0] - EXTRA
    top = pack[:half, :]
    corner = jnp.concatenate([pack[half:last, :half], pack[half:last, half:]], axis=0)
    factor = limit / jnp.maximum(jnp.sqrt(pack[last : last + 1, 0:1]), limit)
    factor_out[...] = jnp.broadcast_to(factor, factor_out.shape)
    gram = jnp.concatenate(
        [top, jnp.concatenate([top[:, half:].T, corner], axis=1)], axis=0
    )
    size = gram.shape[0]
    identity = (
        lax.broadcasted_iota(jnp.int32, (size, size), 0)
        == lax.broadcasted_iota(jnp.int32, (size, size), 1)
    ).astype(jnp.float32)
    trace = jnp.sum(jnp.sum(gram * identity, axis=1, keepdims=True), axis=0, keepdims=True)
    squared = factor * factor
    scale = squared / (squared * jnp.sqrt(trace) + norm_epsilon)
    frame = rows[...] * scale
    gram = gram * (scale * scale)
    for sweep in range(NS_STEPS):
        square = three_pass(gram, gram)
        poly = quintic_one * identity + quintic_two * gram + quintic_three * square
        if sweep + 1 < NS_STEPS:
            frame = three_pass(frame, poly)
            gram = three_pass(poly, three_pass(gram, poly))
    block = size // (2 * members)
    order = [c * members + y for y in range(members) for c in range(2)]
    poly = jnp.concatenate([poly[:, k * block : (k + 1) * block] for k in order], axis=1)
    frame = three_pass(frame, poly)
    for t in range(pieces.shape[0] // 2):
        for core in range(2):
            pieces[2 * t + core] = frame[core * PIECE : (core + 1) * PIECE, :]


def frames_kernel(pieces, attention, up, down):
    for m in range(attention.shape[0]):
        attention[m] = pieces[m, : attention.shape[1], :]
    slot = attention.shape[0]
    up[...] = pieces[slot, : up.shape[0], :]
    for k in range(down.shape[0] // PIECE):
        down[k * PIECE : (k + 1) * PIECE, :] = pieces[slot + 1 + k]


def update_kernel(core, line, *refs):
    ab, ub, db, step_attention, step_up, step_down_t, whole = refs[-7:]
    count = (len(refs) - 7) // 2
    own, other = refs[:count], refs[count : 2 * count]
    block = own[0].shape[0]
    mine = core[0]
    for shift in range(count):
        row = 2 * lax.rem(line[0] + (count - shift), count)
        whole[pl.ds(pl.multiple_of((row + mine) * block, block), block), :] = own[shift][...]
        whole[pl.ds(pl.multiple_of((row + 1 - mine) * block, block), block), :] = other[shift][...]
    value = whole[...]
    column = 0
    heads = ab.shape[0]
    width = step_attention.shape[2]
    for m in range(heads):
        step_attention[m] = galore_scale * three_pass(ab[m], value[:, column : column + width])
        column += width
    width = step_up.shape[1]
    step_up[...] = galore_scale * three_pass(ub[...], value[:, column : column + width])
    column += width
    width = step_down_t.shape[0]
    part = value[:, column : column + width]
    step_down_t[...] = galore_scale * three_pass(part, db[...], CONTRACT_MIXED)


def shape_of(*shape):
    return jax.ShapeDtypeStruct(shape, jnp.float32)


def call(kernel, operands, outs, scratch=(), scalars=0, fetch=False, after=()):
    single = not isinstance(outs, (tuple, list))
    out_list = [outs] if single else list(outs)
    moved = sum(4 * math.prod(o.shape) for o in out_list)
    moved += sum(o.dtype.itemsize * o.size for o in operands)
    specs = [HBM if fetch else VMEM] * len(operands)
    specs[:scalars] = [SMEM] * scalars
    count = len(operands)
    operands = (*operands, *after)
    specs = specs + [pl.BlockSpec(memory_space=pl.ANY)] * len(after)

    def body(*refs):
        kernel(*refs[:count], *refs[count + len(after) :])

    return pl.pallas_call(
        body,
        out_shape=outs,
        in_specs=specs,
        out_specs=VMEM if single else [VMEM] * len(out_list),
        scratch_shapes=list(scratch),
        compiler_params=pltpu.CompilerParams(vmem_limit_bytes=(60 if fetch else 32) << 20),
        cost_estimate=pl.CostEstimate(flops=0, bytes_accessed=moved, transcendentals=0),
    )(*operands)


def sum_over(value, axis, masks):
    total = value
    for mask in masks:
        pairs = [(k, k ^ mask) for k in range(lax.axis_size(axis))]
        total = total + lax.ppermute(value, axis, pairs)
    return total


def exchange(value, axes):
    return lax.all_to_all(value, axes, split_axis=0, concat_axis=0, tiled=True)


def on_device(ag, ug, dg, ab, ub, db, am, ap, um, up, dm, dp, vg, vm, vp):
    heads, rows, width = ag.shape
    rank = ab.shape[2]
    block = am.shape[1]
    columns = heads * width + ug.shape[1] + dg.shape[1]
    padded = -(-(columns + 1) // 128) * 128
    tensors = lax.axis_size("x")
    planes = lax.axis_size("z")
    members = lax.axis_size("y")
    owners = tensors * lax.axis_size("c")
    entries = (ag.size + ug.size + dg.size + vg.size) * planes * members * owners
    limit = float(clip_rms * math.sqrt(entries))
    core = lax.axis_index("c").astype(jnp.int32).reshape(1)
    line = lax.axis_index("y").astype(jnp.int32).reshape(1)
    f32 = jnp.float32

    dg_t = dg.T
    first_operands = (ag, ug, dg_t, ab, ub, db, vg)
    keep, send, wide = call(
        project_kernel,
        (core, *first_operands),
        (
            shape_of(members, block, padded),
            shape_of(members, block, padded),
            shape_of(2 * rows, heads * width + ug.shape[1]),
        ),
        scratch=[pltpu.VMEM((rank, padded), f32)]
        + [pltpu.VMEM(o.shape, o.dtype) for o in first_operands]
        + [pltpu.SemaphoreType.DMA((len(first_operands),))],
        scalars=1,
        fetch=True,
    )
    swap = [(0, 1), (1, 0)]

    send = lax.ppermute(send, "c", swap)
    wide = lax.ppermute(wide, "c", swap)
    chip, squares = chip_sum(columns, keep, send)
    scattered = exchange(chip, "y")
    near = [k for k in range(1, min(4, planes))]
    far = [12, 4] if planes == 16 else [1 << k for k in range(2, planes.bit_length() - 1)]
    squares = sum_over(squares, "z", near)
    sums, copies = call(
        sum_kernel,
        (scattered,),
        (shape_of(block, padded), shape_of(members, block, padded)),
        after=(squares, wide),
    )
    own = exchange(copies, "y")
    squares = sum_over(squares, "x", range(1, tensors))
    pieces = call(
        subspace_kernel,
        (core, own, ag, ug, dg_t, wide),
        shape_of(owners, 2 * PIECE, rank // 2),
        scalars=1,
        after=(squares,),
    )
    for mask in far:
        squares = sum_over(squares, "z", [mask])
    parts = exchange(pieces, OWNERS)
    packed_rows = 3 * rank // 4 + EXTRA
    own_rows, packed = call(
        gram_kernel,
        (parts, squares),
        (shape_of(2 * PIECE, rank), shape_of(packed_rows, rank)),
    )
    first = owners - 3
    places = [(s % 2) * tensors + s // 2 for s in range(first, owners)]
    ring = [(places[k], places[(k + 1) % 3]) for k in range(3)]
    back = [(b, a) for a, b in ring]
    second = lax.ppermute(packed, ("c", "x"), ring)
    third = lax.ppermute(packed, ("c", "x"), back)
    grams = call(spread_kernel, (packed, second, third), shape_of(members, packed_rows, rank))
    grams = exchange(grams, "y")

    def refine_body(*refs):
        refine_kernel(limit, members, *refs)

    frames, factor = call(
        refine_body,
        (grams, own_rows),
        (shape_of(owners, PIECE, rank), shape_of(8, 128)),
    )
    frames = exchange(frames, OWNERS)
    normed, am2, ap2, um2, up2, dm2, dp2, vs2, vm2, vp2 = call(
        moments_kernel,
        (factor, sums, am, ap, um, up, dm, dp, vg, vm, vp),
        [shape_of(block, padded)]
        + [shape_of(*v.shape) for v in (am, ap, um, up, dm, dp, vg, vm, vp)],
    )
    own_normed = [normed]
    for shift in range(1, members):
        pairs = [(k, (k + shift) % members) for k in range(members)]
        own_normed.append(lax.ppermute(normed, "y", pairs))
    other_normed = [lax.ppermute(value, "c", swap) for value in own_normed]
    step_attention, step_up, step_down_t = call(
        update_kernel,
        (core, line, *own_normed, *other_normed, ab, ub, db),
        [shape_of(*v.shape) for v in (ag, ug, dg_t)],
        scratch=[pltpu.VMEM((rank, padded), f32)],
        scalars=2,
    )
    basis_attention, basis_up, basis_down = call(
        frames_kernel,
        (frames,),
        [shape_of(*v.shape) for v in (ab, ub, db)],
    )
    return (
        step_attention, step_up, step_down_t.T,
        am2, ap2, um2, up2, dm2, dp2,
        basis_attention, basis_up, basis_down,
        vs2, vm2, vp2,
    )


def solution(mesh):
    tensors = mesh.shape["tensor"]
    split = Mesh(mesh.devices.reshape(-1, 4, 2, tensors), SHARD_TENSOR)
    stacked = P(None, SHARD, "x")
    flat = P(SHARD, "x")
    vector = P(None, SHARD_TENSOR)
    bases = (P(None, SHARD, None), P(SHARD, None), P(SHARD, None))
    moments = (stacked, stacked, flat, flat, flat, flat)
    in_specs = (stacked, flat, flat) + bases + moments + (vector,) * 3
    out_specs = (stacked, flat, flat) + moments + bases + (vector,) * 3
    return jax.shard_map(
        on_device, mesh=split, in_specs=in_specs, out_specs=out_specs, check_vma=False
    )
```

```python
import math

import jax
import jax.numpy as jnp
from jax import lax
from jax.experimental import pallas as pl
from jax.experimental.pallas import tpu as pltpu
from jax.sharding import Mesh
from jax.sharding import PartitionSpec as P

NS_STEPS = 3
STEP = 10
SHARD = ("z", "y", "c")
SHARD_TENSOR = ("z", "y", "c", "x")
OWNERS = ("x", "c")
PIECE = 128
EXTRA = 8
VMEM = pl.BlockSpec(memory_space=pltpu.VMEM)
HBM = pl.BlockSpec(memory_space=pltpu.HBM)
SMEM = pl.BlockSpec(memory_space=pltpu.SMEM)

quintic_one = 3.4445
quintic_two = -4.775
quintic_three = 2.0315
decay_first = 0.9
decay_second = 0.95
adam_epsilon = 1e-08
norm_epsilon = 1e-07
galore_scale = 0.25
clip_rms = 1.0

CONTRACT_FIRST = (((0,), (0,)), ((), ()))
CONTRACT_LAST = (((1,), (1,)), ((), ()))
CONTRACT_MIXED = (((0,), (1,)), ((), ()))
CONTRACT_PLAIN = (((1,), (0,)), ((), ()))


def highest(left, right, dims=CONTRACT_PLAIN):
    return lax.dot_general(
        left, right, dims, precision=lax.Precision.HIGHEST, preferred_element_type=jnp.float32
    )


def halves_of(value):
    first = value.astype(jnp.bfloat16)
    return first, (value - first.astype(jnp.float32)).astype(jnp.bfloat16)


def three_pass(left, right, dims=CONTRACT_PLAIN):
    first, second = halves_of(left)
    third, fourth = halves_of(right)

    def dot(one, two):
        return lax.dot_general(one, two, dims, preferred_element_type=jnp.float32)

    return dot(first, third) + (dot(first, fourth) + dot(second, third))


def thirds(value):
    first = value.astype(jnp.bfloat16)
    rest = value - first.astype(jnp.float32)
    second = rest.astype(jnp.bfloat16)
    third = (rest - second.astype(jnp.float32)).astype(jnp.bfloat16)
    return first, second, third


def exact_left(value, gradient, dims):
    total = None
    for term in reversed(thirds(value)):
        product = lax.dot_general(term, gradient, dims, preferred_element_type=jnp.float32)
        total = product if total is None else total + product
    return total


def exact_right(gradient, value, dims):
    total = None
    for term in reversed(thirds(value)):
        product = lax.dot_general(gradient, term, dims, preferred_element_type=jnp.float32)
        total = product if total is None else total + product
    return total


def adam_moments(gradient, mean_now, power_now):
    mean_next = decay_first * mean_now + (1.0 - decay_first) * gradient
    power_next = decay_second * power_now + (1.0 - decay_second) * gradient * gradient
    fix_first = 1.0 - decay_first**STEP
    fix_second = 1.0 - decay_second**STEP
    normed = mean_next / fix_first / (jnp.sqrt(power_next / fix_second) + adam_epsilon)
    return (normed, mean_next, power_next)


def square_sum(value):
    return jnp.sum(jnp.sum(value * value, axis=1, keepdims=True), axis=0, keepdims=True)


def project_kernel(core, *refs):
    count = 7
    sources = refs[:count]
    keep, send, wide, whole = refs[count : count + 4]
    held = refs[count + 4 : count + 4 + count]
    done = refs[-1]
    copies = [
        pltpu.make_async_copy(source, target, done.at[index])
        for index, (source, target) in enumerate(zip(sources, held))
    ]
    for copy in copies:
        copy.start()
    ag, ug, dg_t, ab, ub, db, vg = held
    heads = ag.shape[0]
    for index in (0, 3):
        copies[index].wait()
    parts = []
    wides = []
    rows = ug.shape[0]
    squares = jnp.zeros((1, 1), jnp.float32)
    for m in range(heads):
        gradient = ag[m]
        parts.append(exact_left(ab[m], gradient, CONTRACT_FIRST))
        wides.append(gradient.astype(jnp.float32))
        squares = squares + square_sum(wides[-1])
    for index in (1, 4):
        copies[index].wait()
    gradient = ug[...]
    parts.append(exact_left(ub[...], gradient, CONTRACT_FIRST))
    wides.append(gradient.astype(jnp.float32))
    squares = squares + square_sum(wides[-1])
    wide[:rows, :] = jnp.concatenate(wides, axis=1)
    for index in (2, 5, 6):
        copies[index].wait()
    gradient = dg_t[...]
    parts.append(exact_left(db[...], gradient, CONTRACT_MIXED))
    lower = gradient.astype(jnp.float32)
    for k in range(lower.shape[0] // rows):
        start = k * lower.shape[1]
        wide[rows:, start : start + lower.shape[1]] = lower[k * rows : (k + 1) * rows, :]
    squares = squares + square_sum(lower) + square_sum(vg[...])
    column = sum(part.shape[1] for part in parts)
    parts.append(jnp.broadcast_to(squares, (whole.shape[0], whole.shape[1] - column)))
    whole[...] = jnp.concatenate(parts, axis=1)
    block = keep.shape[1]
    mine = core[0]
    for row in range(keep.shape[0]):
        keep[row] = whole[pl.ds(pl.multiple_of((2 * row + mine) * block, block), block), :]
        send[row] = whole[pl.ds(pl.multiple_of((2 * row + 1 - mine) * block, block), block), :]


def chip_kernel(column, keep, received, chip, squares):
    value = keep[...] + received[...]
    chip[...] = value
    squares[...] = jnp.broadcast_to(value[0, 0:1, column : column + 1], squares.shape)


def chip_sum(column, keep, received):
    count, block, padded = keep.shape
    spec = pl.BlockSpec((1, block, padded), lambda i: (i, 0, 0))

    def body(*refs):
        chip_kernel(column, *refs)

    return pl.pallas_call(
        body,
        out_shape=(shape_of(*keep.shape), shape_of(8, 128)),
        grid=(count,),
        in_specs=[spec, spec],
        out_specs=[spec, pl.BlockSpec((8, 128), lambda i: (0, 0))],
        compiler_params=pltpu.CompilerParams(vmem_limit_bytes=16 << 20),
        cost_estimate=pl.CostEstimate(
            flops=0, bytes_accessed=12 * keep.size, transcendentals=0
        ),
    )(keep, received)


def sum_kernel(parts, total, copies):
    value = parts[0]
    for row in range(1, parts.shape[0]):
        value = value + parts[row]
    total[...] = value
    for row in range(copies.shape[0]):
        copies[row] = value


def moments_kernel(
    factor, sums, am, ap, um, up, dm, dp, vg, vm, vp,
    normed, am_out, ap_out, um_out, up_out, dm_out, dp_out, vs_out, vm_out, vp_out,
):
    scale = factor[0:1, 0:1]
    heads = am.shape[0]
    width = am.shape[2]
    column = 0
    parts = []
    value = sums[...] * scale
    for m in range(heads):
        step, mean, power = adam_moments(value[:, column : column + width], am[m], ap[m])
        parts.append(step)
        am_out[m] = mean
        ap_out[m] = power
        column += width
    for mean_now, power_now, mean_out, power_out in (
        (um, up, um_out, up_out), (dm, dp, dm_out, dp_out)
    ):
        width = mean_now.shape[1]
        step, mean, power = adam_moments(
            value[:, column : column + width], mean_now[...], power_now[...]
        )
        parts.append(step)
        mean_out[...] = mean
        power_out[...] = power
        column += width
    parts.append(jnp.zeros((value.shape[0], value.shape[1] - column), jnp.float32))
    normed[...] = jnp.concatenate(parts, axis=1)
    step, mean, power = adam_moments(vg[...] * scale, vm[...], vp[...])
    vs_out[...] = step
    vm_out[...] = mean
    vp_out[...] = power


def subspace_kernel(core, halves, ag, ug, dg_t, wide, pieces):
    mine = core[0]
    value = jnp.concatenate([halves[row] for row in range(halves.shape[0])], axis=0)
    heads, rows, width = ag.shape
    there = wide[...].astype(jnp.bfloat16)
    tall = dg_t.shape[1]
    both = [
        jnp.concatenate([ag[m], there[:rows, m * width : (m + 1) * width]], axis=0)
        for m in range(heads)
    ]
    both.append(jnp.concatenate([ug[...], there[:rows, heads * width :]], axis=0))
    lower = [there[rows:, k * tall : (k + 1) * tall] for k in range(dg_t.shape[0] // rows)]
    both.append(jnp.concatenate([dg_t[...], jnp.concatenate(lower, axis=0)], axis=1))
    places = [pl.multiple_of(place * PIECE, PIECE) for place in (mine, 1 - mine)]
    slot = 0
    column = 0
    for index, gradient in enumerate(both):
        dims = CONTRACT_MIXED if index == heads + 1 else CONTRACT_LAST
        columns = gradient.shape[0] if index == heads + 1 else gradient.shape[1]
        product = exact_right(gradient, value[:, column : column + columns], dims)
        column += columns
        size = product.shape[0] // 2
        for start in range(0, size, PIECE):
            stop = min(size, start + PIECE)
            for k, place in enumerate(places):
                part = product[k * size + start : k * size + stop]
                if stop - start < PIECE:
                    gap = jnp.zeros((PIECE - stop + start, product.shape[1]), jnp.float32)
                    part = jnp.concatenate([part, gap], axis=0)
                pieces[slot, pl.ds(place, PIECE), :] = part
            slot += 1


def gram_kernel(parts, squares, rows_out, packed):
    tensors = parts.shape[0] // 2
    halves = []
    for core in range(2):
        value = parts[core]
        for t in range(1, tensors):
            value = value + parts[2 * t + core]
        halves.append(value)
    rows = jnp.concatenate(halves, axis=1)
    rows_out[...] = rows
    gram = highest(rows, rows, CONTRACT_FIRST)
    half = gram.shape[0] // 2
    last = half + half // 2
    packed[:half, :] = gram[:half, :]
    packed[half:last, :half] = gram[half:last, half:]
    packed[half:last, half:] = gram[last:, half:]
    packed[last:, :] = jnp.broadcast_to(squares[0:1, 0:1], (EXTRA, packed.shape[1]))


def spread_kernel(first, second, third, copies):
    size = first.shape[0] - EXTRA
    value = first[:size, :] + (second[:size, :] + third[:size, :])
    for row in range(copies.shape[0]):
        copies[row, :size, :] = value
        copies[row, size:, :] = first[size:, :]


def refine_kernel(limit, members, packs, rows, pieces, factor_out):
    pack = packs[0]
    for row in range(1, packs.shape[0]):
        pack = pack + packs[row]
    half = pack.shape[1] // 2
    last = pack.shape[0] - EXTRA
    top = pack[:half, :]
    corner = jnp.concatenate([pack[half:last, :half], pack[half:last, half:]], axis=0)
    factor = limit / jnp.maximum(jnp.sqrt(pack[last : last + 1, 0:1]), limit)
    factor_out[...] = jnp.broadcast_to(factor, factor_out.shape)
    gram = jnp.concatenate(
        [top, jnp.concatenate([top[:, half:].T, corner], axis=1)], axis=0
    )
    size = gram.shape[0]
    identity = (
        lax.broadcasted_iota(jnp.int32, (size, size), 0)
        == lax.broadcasted_iota(jnp.int32, (size, size), 1)
    ).astype(jnp.float32)
    trace = jnp.sum(jnp.sum(gram * identity, axis=1, keepdims=True), axis=0, keepdims=True)
    squared = factor * factor
    scale = squared / (squared * jnp.sqrt(trace) + norm_epsilon)
    frame = rows[...] * scale
    gram = gram * (scale * scale)
    for sweep in range(NS_STEPS):
        square = three_pass(gram, gram)
        poly = quintic_one * identity + quintic_two * gram + quintic_three * square
        if sweep + 1 < NS_STEPS:
            frame = three_pass(frame, poly)
            gram = three_pass(poly, three_pass(gram, poly))
    block = size // (2 * members)
    order = [c * members + y for y in range(members) for c in range(2)]
    poly = jnp.concatenate([poly[:, k * block : (k + 1) * block] for k in order], axis=1)
    frame = three_pass(frame, poly)
    for t in range(pieces.shape[0] // 2):
        for core in range(2):
            pieces[2 * t + core] = frame[core * PIECE : (core + 1) * PIECE, :]


def frames_kernel(pieces, attention, up, down):
    for m in range(attention.shape[0]):
        attention[m] = pieces[m, : attention.shape[1], :]
    slot = attention.shape[0]
    up[...] = pieces[slot, : up.shape[0], :]
    for k in range(down.shape[0] // PIECE):
        down[k * PIECE : (k + 1) * PIECE, :] = pieces[slot + 1 + k]


def update_kernel(core, line, *refs):
    ab, ub, db, step_attention, step_up, step_down_t, whole = refs[-7:]
    count = (len(refs) - 7) // 2
    own, other = refs[:count], refs[count : 2 * count]
    block = own[0].shape[0]
    mine = core[0]
    for shift in range(count):
        row = 2 * lax.rem(line[0] + (count - shift), count)
        whole[pl.ds(pl.multiple_of((row + mine) * block, block), block), :] = own[shift][...]
        whole[pl.ds(pl.multiple_of((row + 1 - mine) * block, block), block), :] = other[shift][...]
    value = whole[...]
    column = 0
    heads = ab.shape[0]
    width = step_attention.shape[2]
    for m in range(heads):
        step_attention[m] = galore_scale * three_pass(ab[m], value[:, column : column + width])
        column += width
    width = step_up.shape[1]
    step_up[...] = galore_scale * three_pass(ub[...], value[:, column : column + width])
    column += width
    width = step_down_t.shape[0]
    part = value[:, column : column + width]
    step_down_t[...] = galore_scale * three_pass(part, db[...], CONTRACT_MIXED)


def shape_of(*shape):
    return jax.ShapeDtypeStruct(shape, jnp.float32)


def call(kernel, operands, outs, scratch=(), scalars=0, fetch=False, after=()):
    single = not isinstance(outs, (tuple, list))
    out_list = [outs] if single else list(outs)
    moved = sum(4 * math.prod(o.shape) for o in out_list)
    moved += sum(o.dtype.itemsize * o.size for o in operands)
    specs = [HBM if fetch else VMEM] * len(operands)
    specs[:scalars] = [SMEM] * scalars
    count = len(operands)
    operands = (*operands, *after)
    specs = specs + [pl.BlockSpec(memory_space=pl.ANY)] * len(after)

    def body(*refs):
        kernel(*refs[:count], *refs[count + len(after) :])

    return pl.pallas_call(
        body,
        out_shape=outs,
        in_specs=specs,
        out_specs=VMEM if single else [VMEM] * len(out_list),
        scratch_shapes=list(scratch),
        compiler_params=pltpu.CompilerParams(vmem_limit_bytes=(60 if fetch else 32) << 20),
        cost_estimate=pl.CostEstimate(flops=0, bytes_accessed=moved, transcendentals=0),
    )(*operands)


def sum_over(value, axis, masks):
    total = value
    for mask in masks:
        pairs = [(k, k ^ mask) for k in range(lax.axis_size(axis))]
        total = total + lax.ppermute(value, axis, pairs)
    return total


def exchange(value, axes):
    return lax.all_to_all(value, axes, split_axis=0, concat_axis=0, tiled=True)


def on_device(ag, ug, dg, ab, ub, db, am, ap, um, up, dm, dp, vg, vm, vp):
    heads, rows, width = ag.shape
    rank = ab.shape[2]
    block = am.shape[1]
    columns = heads * width + ug.shape[1] + dg.shape[1]
    padded = -(-(columns + 1) // 128) * 128
    tensors = lax.axis_size("x")
    planes = lax.axis_size("z")
    members = lax.axis_size("y")
    owners = tensors * lax.axis_size("c")
    entries = (ag.size + ug.size + dg.size + vg.size) * planes * members * owners
    limit = float(clip_rms * math.sqrt(entries))
    core = lax.axis_index("c").astype(jnp.int32).reshape(1)
    line = lax.axis_index("y").astype(jnp.int32).reshape(1)
    f32 = jnp.float32

    dg_t = dg.T
    first_operands = (ag, ug, dg_t, ab, ub, db, vg)
    keep, send, wide = call(
        project_kernel,
        (core, *first_operands),
        (
            shape_of(members, block, padded),
            shape_of(members, block, padded),
            shape_of(2 * rows, heads * width + ug.shape[1]),
        ),
        scratch=[pltpu.VMEM((rank, padded), f32)]
        + [pltpu.VMEM(o.shape, o.dtype) for o in first_operands]
        + [pltpu.SemaphoreType.DMA((len(first_operands),))],
        scalars=1,
        fetch=True,
    )
    swap = [(0, 1), (1, 0)]

    send = lax.ppermute(send, "c", swap)
    wide = lax.ppermute(wide, "c", swap)
    chip, squares = chip_sum(columns, keep, send)
    scattered = exchange(chip, "y")
    near = [k for k in range(1, min(4, planes))]
    far = [12, 4] if planes == 16 else [1 << k for k in range(2, planes.bit_length() - 1)]
    squares = sum_over(squares, "z", near)
    sums, copies = call(
        sum_kernel,
        (scattered,),
        (shape_of(block, padded), shape_of(members, block, padded)),
        after=(squares, wide),
    )
    own = exchange(copies, "y")
    squares = sum_over(squares, "x", range(1, tensors))
    pieces = call(
        subspace_kernel,
        (core, own, ag, ug, dg_t, wide),
        shape_of(owners, 2 * PIECE, rank // 2),
        scalars=1,
        after=(squares,),
    )
    for mask in far:
        squares = sum_over(squares, "z", [mask])
    parts = exchange(pieces, OWNERS)
    packed_rows = 3 * rank // 4 + EXTRA
    own_rows, packed = call(
        gram_kernel,
        (parts, squares),
        (shape_of(2 * PIECE, rank), shape_of(packed_rows, rank)),
    )
    first = owners - 3
    places = [(s % 2) * tensors + s // 2 for s in range(first, owners)]
    ring = [(places[k], places[(k + 1) % 3]) for k in range(3)]
    back = [(b, a) for a, b in ring]
    second = lax.ppermute(packed, ("c", "x"), ring)
    third = lax.ppermute(packed, ("c", "x"), back)
    grams = call(spread_kernel, (packed, second, third), shape_of(members, packed_rows, rank))
    grams = exchange(grams, "y")

    def refine_body(*refs):
        refine_kernel(limit, members, *refs)

    frames, factor = call(
        refine_body,
        (grams, own_rows),
        (shape_of(owners, PIECE, rank), shape_of(8, 128)),
    )
    frames = exchange(frames, OWNERS)
    normed, am2, ap2, um2, up2, dm2, dp2, vs2, vm2, vp2 = call(
        moments_kernel,
        (factor, sums, am, ap, um, up, dm, dp, vg, vm, vp),
        [shape_of(block, padded)]
        + [shape_of(*v.shape) for v in (am, ap, um, up, dm, dp, vg, vm, vp)],
    )
    own_normed = [normed]
    for shift in range(1, members):
        pairs = [(k, (k + shift) % members) for k in range(members)]
        own_normed.append(lax.ppermute(normed, "y", pairs))
    other_normed = [lax.ppermute(value, "c", swap) for value in own_normed]
    basis_attention, basis_up, basis_down = call(
        frames_kernel,
        (frames,),
        [shape_of(*v.shape) for v in (ab, ub, db)],
    )
    step_attention, step_up, step_down_t = call(
        update_kernel,
        (core, line, *own_normed, *other_normed, ab, ub, db),
        [shape_of(*v.shape) for v in (ag, ug, dg_t)],
        scratch=[pltpu.VMEM((rank, padded), f32)],
        scalars=2,
        after=(basis_up,),
    )
    return (
        step_attention, step_up, step_down_t.T,
        am2, ap2, um2, up2, dm2, dp2,
        basis_attention, basis_up, basis_down,
        vs2, vm2, vp2,
    )


def solution(mesh):
    tensors = mesh.shape["tensor"]
    split = Mesh(mesh.devices.reshape(-1, 4, 2, tensors), SHARD_TENSOR)
    stacked = P(None, SHARD, "x")
    flat = P(SHARD, "x")
    vector = P(None, SHARD_TENSOR)
    bases = (P(None, SHARD, None), P(SHARD, None), P(SHARD, None))
    moments = (stacked, stacked, flat, flat, flat, flat)
    in_specs = (stacked, flat, flat) + bases + moments + (vector,) * 3
    out_specs = (stacked, flat, flat) + moments + bases + (vector,) * 3
    return jax.shard_map(
        on_device, mesh=split, in_specs=in_specs, out_specs=out_specs, check_vma=False
    )
```
